128 devices in a mesh: grp: 2 (over core), vocab: 32 (over x_hi, y, z), seq: 2 (over x_lo).
Axes of the slice: x: 4 (x_hi: 2, x_lo: 2; x = x_hi * 2 + x_lo), y: 4, z: 4, core: 2. Of those that a mesh axis runs over, the one named last changes fastest.
Arguments:
- teacher_rows: bfloat16 [256, 8192], P('vocab', ('grp', 'seq')), may hold values from -104 to 104
- student_rows: bfloat16 [256, 4096], P(('grp', 'vocab')), may hold values from -104 to 104
- teacher_head: bfloat16 [8192, 2, 64128], P(('grp', 'seq'), None, 'vocab'), may hold values from -0.0625 to 0.0625
- student_head: bfloat16 [4096, 128256], P(None, ('grp', 'vocab', 'seq')), may hold values from -0.09375 to 0.09375
- targets: int32 [256], replicated, may hold values from 0 to 128255
- loss_grad: float32 [256], replicated, may hold values from 10 to 100
Outputs:
- hidden_grad: bfloat16 [256, 4096], P(('grp', 'vocab', 'seq'))
- token_loss: float32 [256], replicated
The draws below stay inside these ranges and needn't reach their ends.
All inputs are finite; a program needn't handle non-finite values.
Results may differ from the reference program's by a relative error of at most 0.014.
Values may be sent and summed in bfloat16 or wider, within the bound.
No kernel may reach another device: no remote copies, remote signals or barrier semaphores. Data moves between devices by JAX's collectives and lax.ppermute only.
A program may use at most 128 MiB of HBM per device.

```python
import math
import jax
import jax.numpy as jnp
from jax import lax

DT = 8192
DS = 4096
V = 128256
SLAB = 256


def drawn_rows(rng_key, height, breadth, level):
    values = jax.random.normal(rng_key, (height, breadth), jnp.float32)
    return level * jnp.clip(values, -5.0, 5.0)


def draw_teacher_rows(key, part):
    key = jax.random.fold_in(key, 11)
    return drawn_rows(key, SLAB, DT, 3.0).astype(jnp.bfloat16)


def draw_student_rows(key, part):
    key = jax.random.fold_in(key, 23)
    return drawn_rows(key, SLAB, DS, 3.0).astype(jnp.bfloat16)


def set_ends(values, own_key, low, largest):
    longest = values.shape.index(max(values.shape))
    spots = []
    for shift in (0, 1):
        where = [jax.random.randint(jax.random.fold_in(own_key, axis), (), 0, length) for axis, length in enumerate(values.shape)]
        where[longest] = (where[longest] + shift) % values.shape[longest]
        spots.append(tuple(where))
    return values.at[spots[0]].set(low).at[spots[1]].set(largest)


def steps_of(own_key, extent, pieces, low, top_value):
    def one(axis_at, parts):
        draws = jax.random.uniform(jax.random.fold_in(jax.random.fold_in(own_key, 6), axis_at), (parts,), jnp.float32, low / len(pieces), top_value / len(pieces))
        return jnp.repeat(jnp.exp(draws), extent[axis_at] // parts).reshape((-1,) + (1,) * (len(extent) - axis_at - 1))

    gain = one(*pieces[0])
    for cut in pieces[1:]:
        gain = gain * one(*cut)
    return gain


def bell_draw(stream_key, dims, scale, reach, pieces=(), kind=jnp.bfloat16):
    entries = jax.random.normal(stream_key, dims, jnp.float32) * scale
    if len(pieces) > 0:
        entries = steps_of(stream_key, dims, pieces, -0.22, 0.18) * entries
    return jnp.clip(entries, min=-reach, max=reach).astype(kind)


def setup_inputs(seed: int = 0) -> dict:
    keys = jax.random.split(jax.random.key(seed), 7)
    return {
        "teacher_rows": draw_teacher_rows(jax.random.fold_in(keys[6], 71), 0),
        "student_rows": draw_student_rows(jax.random.fold_in(keys[6], 71), 0),
        "teacher_head": bell_draw(keys[2], (DT, 2, V // 2), DT ** -0.5, 0.0625, ((0, 4), (2, 32))),
        "student_head": bell_draw(keys[3], (DS, V), DS ** -0.5, 0.09375, ((1, 128),)),
        "targets": set_ends(jax.random.randint(keys[4], (SLAB,), 0, V), jax.random.fold_in(keys[4], 1), 0, V - 1).astype(jnp.int32),
        "loss_grad": jnp.clip(jnp.exp(jax.random.uniform(keys[5], (SLAB,), jnp.float32, math.log(10.0), math.log(100.0))), 10.0, 100.0),
    }


def reference(teacher_rows, student_rows, teacher_head, student_head, targets, loss_grad):
    teacher_logits = jnp.dot(teacher_rows, teacher_head.reshape(DT, V), preferred_element_type=jnp.float32)
    student_logits = jnp.dot(student_rows, student_head, preferred_element_type=jnp.float32)
    teacher_norm = jax.nn.logsumexp(teacher_logits, axis=1)
    student_norm = jax.nn.logsumexp(student_logits, axis=1)
    teacher_probs = jnp.exp(teacher_logits - teacher_norm[:, None])
    student_probs = jnp.exp(student_logits - student_norm[:, None])
    columns = jnp.arange(V, dtype=jnp.int32)
    onehot = targets[:, None] == columns[None, :]
    picked = jnp.sum(jnp.where(onehot, student_logits, jnp.zeros_like(student_logits)), axis=1)
    token_loss = jnp.sum(teacher_probs * (teacher_logits - student_logits), axis=1) - teacher_norm + 2.0 * student_norm - picked
    logit_grad = (loss_grad[:, None] * (2.0 * student_probs - teacher_probs - onehot.astype(jnp.float32))).astype(jnp.bfloat16)
    hidden_grad = lax.dot_general(logit_grad, student_head, (((1,), (1,)), ((), ())), preferred_element_type=jnp.float32)
    return hidden_grad.astype(jnp.bfloat16), token_loss
```

```python
import functools

import jax
import jax.numpy as jnp
from jax import lax
from jax.experimental import pallas as pl
from jax.experimental.pallas import tpu as pltpu
from jax.sharding import PartitionSpec as P

F32 = jnp.float32
BF16 = jnp.bfloat16
BLOCKS = 6
VMEM = pl.BlockSpec(memory_space=pltpu.VMEM)
SMEM = pl.BlockSpec(memory_space=pltpu.SMEM)


def params(mib=48):
    return pltpu.CompilerParams(vmem_limit_bytes=mib * 1024 * 1024)


def call(kernel, out_shape, *args, in_specs=None, scratch=(), mib=48):
    return pl.pallas_call(
        kernel,
        out_shape=out_shape,
        in_specs=in_specs or [VMEM] * len(args),
        out_specs=jax.tree.map(lambda _: VMEM, out_shape),
        scratch_shapes=scratch,
        compiler_params=params(mib),
    )(*args)


def swap_xhi(a):
    return lax.ppermute(a, "vocab", [(i, i ^ 16) for i in range(32)])


def from_z(a, k):
    return lax.ppermute(a, "vocab", [((i & ~3) | ((i + k) & 3), i) for i in range(32)])


def from_y(a, k):
    return lax.ppermute(a, "vocab", [((i & ~12) | ((i + 4 * k) & 12), i) for i in range(32)])


def from_x(a, bits):
    flip = (bits & 1) | ((bits >> 1) << 5)
    return lax.ppermute(a, ("vocab", "seq"), [(i ^ flip, i) for i in range(64)])


def swap_core(a):
    return lax.ppermute(a, "grp", [(0, 1), (1, 0)])


def swap_seq(a):
    return lax.ppermute(a, "seq", [(0, 1), (1, 0)])


def place_z(pieces, ids):
    def kernel(ids_ref, *refs):
        z = ids_ref[3]
        for k in range(4):
            zk = lax.rem(z + k, 4)
            for h in range(2):
                refs[4][h, zk] = refs[k][h]

    _, n, w = pieces[0].shape
    return call(
        kernel, jax.ShapeDtypeStruct((2, 4, n, w), BF16), ids, *pieces, in_specs=[SMEM] + [VMEM] * 4
    )


def place_y(pieces, ids):
    _, _, n, w = pieces[0].shape
    rows = 4 * n

    def kernel(ids_ref, *refs):
        y = ids_ref[2]
        for k in range(4):
            yk = lax.rem(y + k, 4)
            for h in range(2):
                start = pl.multiple_of(h * 4 * rows + yk * rows, rows)
                refs[4][pl.ds(start, rows), :] = refs[k][h].reshape(rows, w)

    return call(
        kernel, jax.ShapeDtypeStruct((8 * rows, w), BF16), ids, *pieces, in_specs=[SMEM] + [VMEM] * 4
    )


def teacher_part(head, rows, ids, mine, first, count):
    width, _, depth = head.shape
    step = width // (2 * BLOCKS)
    tokens = rows.shape[0]

    def place(i, ids_ref):
        part = ids_ref[1] if mine else 1 - ids_ref[1]
        return (part * BLOCKS + first + i, 0, 0)

    def kernel(ids_ref, w_ref, x_ref, own_ref, other_ref, acc):
        g = ids_ref[0]
        w = w_ref[...].reshape(2 * step, depth)
        out = lax.dot_general(w, x_ref[...], (((1,), (1,)), ((), ())), preferred_element_type=F32)
        for lane in range(tokens // 128):
            cols = slice(lane * 128, lane * 128 + 128)
            acc[lane, 0 : 2 * step, :] = out[:, cols]
            own_ref[0, :, cols] = acc[lane, pl.ds(g, step, stride=2), :]
            other_ref[0, :, cols] = acc[lane, pl.ds(1 - g, step, stride=2), :]

    out = jax.ShapeDtypeStruct((count, step, tokens), F32)
    block = pl.BlockSpec((1, step, tokens), lambda i, r: (i, 0, 0))
    return pl.pallas_call(
        kernel,
        grid_spec=pltpu.PrefetchScalarGridSpec(
            num_scalar_prefetch=1,
            grid=(count,),
            in_specs=[
                pl.BlockSpec((step, 2, depth), place),
                pl.BlockSpec((tokens, depth), lambda i, r: (0, 0)),
            ],
            out_specs=[block, block],
            scratch_shapes=[pltpu.VMEM((tokens // 128, 2 * step + 18, 128), F32)],
        ),
        out_shape=[out, out],
        compiler_params=params(),
        cost_estimate=pl.CostEstimate(
            flops=4 * count * step * depth * tokens,
            bytes_accessed=count * step * depth * 4 + tokens * depth * 2,
            transcendentals=0,
        ),
    )(ids, head, rows)


def student_product(head, own, other, ids):
    width, depth = head.shape
    half = own.shape[0]
    block = 256

    def kernel(ids_ref, w_ref, own_ref, other_ref, out_ref, xs):
        @pl.when(pl.program_id(0) == 0)
        def _():
            g = ids_ref[0]
            xs[pl.ds(pl.multiple_of(g * half, half), half), :] = own_ref[...]
            xs[pl.ds(pl.multiple_of((1 - g) * half, half), half), :] = other_ref[...]

        out_ref[...] = lax.dot_general(
            w_ref[...], xs[...], (((1,), (1,)), ((), ())), preferred_element_type=F32
        )

    rows = pl.BlockSpec((half, depth), lambda i, r: (0, 0))
    return pl.pallas_call(
        kernel,
        grid_spec=pltpu.PrefetchScalarGridSpec(
            num_scalar_prefetch=1,
            grid=(pl.cdiv(width, block),),
            in_specs=[pl.BlockSpec((block, depth), lambda i, r: (i, 0)), rows, rows],
            out_specs=pl.BlockSpec((block, 2 * half), lambda i, r: (i, 0)),
            scratch_shapes=[pltpu.VMEM((2 * half, depth), BF16)],
        ),
        out_shape=jax.ShapeDtypeStruct((width, 2 * half), F32),
        compiler_params=params(),
        cost_estimate=pl.CostEstimate(
            flops=4 * width * depth * half, bytes_accessed=2 * width * depth, transcendentals=0
        ),
    )(ids, head, own, other)


def hits(ids_ref, targets_ref, shape):
    columns = ids_ref[4] + lax.broadcasted_iota(jnp.int32, shape, 0)
    return columns == targets_ref[...]


def local_stats(mine, core, near, student, targets, ids):
    width, tokens = student.shape
    step = width // BLOCKS

    def kernel(ids_ref, mine_ref, core_ref, *refs):
        near_refs = refs[: len(near)]
        s_ref, t_ref, tl_ref, out_ref = refs[len(near) :]
        b = 0
        for ref in near_refs:
            for i in range(ref.shape[0]):
                tl_ref[b * step : (b + 1) * step, :] = (mine_ref[b] + core_ref[b]) + ref[i]
                b += 1
        t, s = tl_ref[...], s_ref[...]
        t_top = jnp.max(t, axis=0, keepdims=True)
        s_top = jnp.max(s, axis=0, keepdims=True)
        e = jnp.exp(t - t_top)
        out_ref[0:1, :] = t_top
        out_ref[1:2, :] = jnp.sum(e, axis=0, keepdims=True)
        out_ref[2:3, :] = jnp.sum(e * (t - s), axis=0, keepdims=True)
        out_ref[3:4, :] = s_top
        out_ref[4:5, :] = jnp.sum(jnp.exp(s - s_top), axis=0, keepdims=True)
        hit = hits(ids_ref, t_ref, s.shape)
        out_ref[5:6, :] = jnp.sum(jnp.where(hit, s, jnp.zeros_like(s)), axis=0, keepdims=True)
        out_ref[6:8, :] = jnp.zeros((2, tokens), F32)

    return call(
        kernel,
        [jax.ShapeDtypeStruct((width, tokens), F32), jax.ShapeDtypeStruct((8, tokens), F32)],
        ids,
        mine,
        core,
        *near,
        student,
        targets,
        in_specs=[SMEM] + [VMEM] * (4 + len(near)),
    )


def merge(stats):
    def kernel(*refs):
        out_ref = refs[-1]
        values = [r[...] for r in refs[:-1]]

        def row(v, i):
            return v[i : i + 1, :]

        for top_row, sums in ((0, (1, 2)), (3, (4,))):
            top = functools.reduce(jnp.maximum, [row(v, top_row) for v in values])
            scale = [jnp.exp(row(v, top_row) - top) for v in values]
            out_ref[top_row : top_row + 1, :] = top
            for i in sums:
                out_ref[i : i + 1, :] = sum(c * row(v, i) for c, v in zip(scale, values))
        out_ref[5:6, :] = sum(row(v, 5) for v in values)
        out_ref[6:8, :] = values[0][6:8, :]

    return call(kernel, jax.ShapeDtypeStruct(stats[0].shape, F32), *stats)


def hidden_part(head, teacher, student, stats, targets, loss_grad, ids):
    width, depth = head.shape
    tokens = teacher.shape[1]
    half = tokens // 2
    block = 1024

    def kernel(ids_ref, w_ref, tl_ref, sl_ref, st_ref, t_ref, g_ref, own_ref, other_ref, grad):
        @pl.when(pl.program_id(0) == 0)
        def _():
            st = st_ref[...]
            t_probs = jnp.exp(tl_ref[...] - st[0:1, :]) / st[1:2, :]
            s_probs = jnp.exp(sl_ref[...] - st[3:4, :]) / st[4:5, :]
            hit = hits(ids_ref, t_ref, t_probs.shape)
            value = g_ref[...] * (2.0 * s_probs - t_probs - hit.astype(F32))
            first = ids_ref[0] == 0
            low, high = value[:, :half].T, value[:, half:].T
            grad[0:half, :] = jnp.where(first, low, high).astype(BF16)
            grad[half:tokens, :] = jnp.where(first, high, low).astype(BF16)

        out = jnp.dot(grad[...], w_ref[...], preferred_element_type=F32)
        own_ref[...] = out[:half]
        other_ref[...] = out[half:].astype(BF16)

    def whole(*shape):
        return pl.BlockSpec(shape, lambda i, r: (0, 0))

    out_block = pl.BlockSpec((half, block), lambda i, r: (0, i))
    return pl.pallas_call(
        kernel,
        grid_spec=pltpu.PrefetchScalarGridSpec(
            num_scalar_prefetch=1,
            grid=(depth // block,),
            in_specs=[
                pl.BlockSpec((width, block), lambda i, r: (0, i)),
                whole(width, tokens),
                whole(width, tokens),
                whole(8, tokens),
                whole(1, tokens),
                whole(1, tokens),
            ],
            out_specs=[out_block, out_block],
            scratch_shapes=[pltpu.VMEM((tokens, width), BF16)],
        ),
        out_shape=[
            jax.ShapeDtypeStruct((half, depth), F32),
            jax.ShapeDtypeStruct((half, depth), BF16),
        ],
        compiler_params=params(),
        cost_estimate=pl.CostEstimate(
            flops=2 * width * depth * tokens, bytes_accessed=2 * width * depth, transcendentals=0
        ),
    )(ids, head, teacher, student, stats, targets, loss_grad)


def body(teacher_rows, student_rows, teacher_head, student_head, targets, loss_grad):
    t_head = jnp.transpose(teacher_head, (2, 1, 0))
    s_head = jnp.transpose(student_head, (1, 0))
    width = s_head.shape[0]
    grp, vocab, seq = lax.axis_index("grp"), lax.axis_index("vocab"), lax.axis_index("seq")
    shard = (grp * lax.axis_size("vocab") + vocab) * lax.axis_size("seq") + seq
    ids = jnp.stack([grp, seq, (vocab // 4) % 4, vocab % 4, shard * width]).astype(jnp.int32)
    lower = vocab < 16
    targets2, loss_grad2 = targets.reshape(1, -1), loss_grad.reshape(1, -1)

    def pair(a):
        b = swap_xhi(a)
        return jnp.where(lower, jnp.stack([a, b]), jnp.stack([b, a]))

    a, b = pair(teacher_rows), pair(student_rows)
    a = place_z([a] + [from_z(a, k) for k in (1, 2, 3)], ids)
    b = place_z([b] + [from_z(b, k) for k in (1, 2, 3)], ids)
    a = place_y([a] + [from_y(a, k) for k in (1, 2, 3)], ids)
    b, a = lax.optimization_barrier((b, a))
    b = place_y([b] + [from_y(b, k) for k in (1, 2, 3)], ids)

    near = []
    for first in (0, 2, 4):
        own, other = teacher_part(t_head, a, ids, False, first, 2)
        near.append(swap_seq(own + swap_core(other)))
    mine, other = teacher_part(t_head, a, ids, True, 0, BLOCKS)
    core = swap_core(other)

    student = student_product(s_head, b, swap_core(b), ids)
    teacher, stats = local_stats(mine, core, near, student, targets2, ids)
    stats = merge([stats, swap_core(stats)])
    stats = merge([stats] + [from_x(stats, k) for k in (1, 2, 3)])
    stats = merge([stats] + [from_y(stats, k) for k in (1, 2, 3)])
    stats = merge([stats] + [from_z(stats, k) for k in (1, 2, 3)])

    own, other = hidden_part(s_head, teacher, student, stats, targets2, loss_grad2, ids)
    part = (own + swap_core(other).astype(F32)).astype(BF16)
    part = part.reshape(64, 2, -1)
    part = lax.all_to_all(part, ("vocab", "seq"), 0, 0, tiled=True)
    hidden = jnp.sum(part.astype(F32), axis=0).astype(BF16)

    t_norm = stats[0] + jnp.log(stats[1])
    s_norm = stats[3] + jnp.log(stats[4])
    token_loss = stats[2] / stats[1] - t_norm + 2.0 * s_norm - stats[5]
    return hidden, token_loss


def solution(mesh):
    return jax.shard_map(
        body,
        mesh=mesh,
        in_specs=(
            P("vocab", ("grp", "seq")),
            P(("grp", "vocab"), None),
            P(("grp", "seq"), None, "vocab"),
            P(None, ("grp", "vocab", "seq")),
            P(),
            P(),
        ),
        out_specs=(P(("grp", "vocab", "seq"), None), P()),
        check_vma=False,
    )
```

```python
import functools

import jax
import jax.numpy as jnp
from jax import lax
from jax.experimental import pallas as pl
from jax.experimental.pallas import tpu as pltpu
from jax.sharding import PartitionSpec as P

F32 = jnp.float32
BF16 = jnp.bfloat16
BLOCKS = 6
TINY = pl.CostEstimate(flops=1000, bytes_accessed=1000, transcendentals=0)
VMEM = pl.BlockSpec(memory_space=pltpu.VMEM)
SMEM = pl.BlockSpec(memory_space=pltpu.SMEM)


def params(mib=20):
    return pltpu.CompilerParams(vmem_limit_bytes=mib * 1024 * 1024)


def call(kernel, out_shape, *args, in_specs=None, scratch=(), mib=20):
    return pl.pallas_call(
        kernel,
        out_shape=out_shape,
        in_specs=in_specs or [VMEM] * len(args),
        out_specs=jax.tree.map(lambda _: VMEM, out_shape),
        scratch_shapes=scratch,
        compiler_params=params(mib),
        cost_estimate=TINY,
    )(*args)


def swap_xhi(a):
    return lax.ppermute(a, "vocab", [(i, i ^ 16) for i in range(32)])


def swap_core(a):
    return lax.ppermute(a, "grp", [(0, 1), (1, 0)])


def swap_seq(a):
    return lax.ppermute(a, "seq", [(0, 1), (1, 0)])


def place(a):
    n, two, m, w = a.shape

    def kernel(in_ref, out_ref):
        for h in range(two):
            out_ref[h * n * m : (h + 1) * n * m, :] = in_ref[:, h].reshape(n * m, w)

    return call(kernel, jax.ShapeDtypeStruct((two * n * m, w), BF16), a)


def teacher_part(head, rows, ids, mine, first, count):
    width, _, depth = head.shape
    step = width // (2 * BLOCKS)
    tokens = rows.shape[0]
    padded = -(-step // 8) * 8

    def kernel(ids_ref, w_hbm, x_ref, own_ref, other_ref, w_buf, acc, sems):
        g = ids_ref[0]
        part = ids_ref[1] if mine else 1 - ids_ref[1]
        copies = []
        for i in range(count):
            start = (part * BLOCKS + first + i) * step
            copies.append(
                pltpu.make_async_copy(w_hbm.at[pl.ds(start, step)], w_buf.at[i], sems.at[i])
            )
        for c in copies:
            c.start()
        for i in range(count):
            copies[i].wait()
            w = w_buf[i].reshape(2 * step, depth)
            out = lax.dot_general(
                w, x_ref[...], (((1,), (1,)), ((), ())), preferred_element_type=F32
            )
            for lane in range(tokens // 128):
                cols = slice(lane * 128, lane * 128 + 128)
                acc[lane, 0 : 2 * step, :] = out[:, cols]
                rows = slice(i * padded, i * padded + step)
                own_ref[rows, cols] = acc[lane, pl.ds(g, step, stride=2), :]
                other_ref[rows, cols] = acc[lane, pl.ds(1 - g, step, stride=2), :]

    out = jax.ShapeDtypeStruct((count * padded, tokens), F32)
    return call(
        kernel,
        [out, out],
        ids,
        head,
        rows,
        in_specs=[SMEM, pl.BlockSpec(memory_space=pl.ANY), VMEM],
        scratch=[
            pltpu.VMEM((count, step, 2, depth), BF16),
            pltpu.VMEM((tokens // 128, 2 * step + 18, 128), F32),
            pltpu.SemaphoreType.DMA((count,)),
        ],
        mib=50,
    )


def student_product(head, own, other, ids):
    width, depth = head.shape
    half = own.shape[0]
    block = 256

    def kernel(ids_ref, w_ref, own_ref, other_ref, out_ref, xs):
        g = ids_ref[0]
        xs[pl.ds(pl.multiple_of(g * half, half), half), :] = own_ref[...]
        xs[pl.ds(pl.multiple_of((1 - g) * half, half), half), :] = other_ref[...]
        for start in range(0, width, block):
            rows = slice(start, min(start + block, width))
            out_ref[rows, :] = lax.dot_general(
                w_ref[rows, :], xs[...], (((1,), (1,)), ((), ())), preferred_element_type=F32
            )

    return call(
        kernel,
        jax.ShapeDtypeStruct((width, 2 * half), F32),
        ids,
        head,
        own,
        other,
        in_specs=[SMEM, VMEM, VMEM, VMEM],
        scratch=[pltpu.VMEM((2 * half, depth), BF16)],
    )


def hits(ids_ref, targets_ref, shape):
    columns = ids_ref[4] + lax.broadcasted_iota(jnp.int32, shape, 0)
    return columns == targets_ref[...]


def local_stats(mine, core, near, student, targets, ids):
    width, tokens = student.shape
    step = width // BLOCKS
    padded = -(-step // 8) * 8

    def kernel(ids_ref, mine_ref, core_ref, *refs):
        near_refs = refs[: len(near)]
        s_ref, t_ref, tl_ref, out_ref = refs[len(near) :]
        b = 0
        for ref in near_refs:
            for i in range(ref.shape[0] // padded):
                here = slice(b * padded, b * padded + step)
                there = slice(i * padded, i * padded + step)
                own = mine_ref[here, :] + core_ref[here, :]
                tl_ref[b * step : (b + 1) * step, :] = own + ref[there, :]
                b += 1
        t, s = tl_ref[...], s_ref[...]
        t_top = jnp.max(t, axis=0, keepdims=True)
        s_top = jnp.max(s, axis=0, keepdims=True)
        e = jnp.exp(t - t_top)
        out_ref[0:1, :] = t_top
        out_ref[1:2, :] = jnp.sum(e, axis=0, keepdims=True)
        out_ref[2:3, :] = jnp.sum(e * (t - s), axis=0, keepdims=True)
        out_ref[3:4, :] = s_top
        out_ref[4:5, :] = jnp.sum(jnp.exp(s - s_top), axis=0, keepdims=True)
        hit = hits(ids_ref, t_ref, s.shape)
        out_ref[5:6, :] = jnp.sum(jnp.where(hit, s, jnp.zeros_like(s)), axis=0, keepdims=True)
        out_ref[6:8, :] = jnp.zeros((2, tokens), F32)

    return call(
        kernel,
        [jax.ShapeDtypeStruct((width, tokens), F32), jax.ShapeDtypeStruct((8, tokens), F32)],
        ids,
        mine,
        core,
        *near,
        student,
        targets,
        in_specs=[SMEM] + [VMEM] * (4 + len(near)),
    )


def merge(stats):
    def kernel(*refs):
        out_ref = refs[-1]
        values = [r[...] for r in refs[:-1]]

        def row(v, i):
            return v[i : i + 1, :]

        for top_row, sums in ((0, (1, 2)), (3, (4,))):
            top = functools.reduce(jnp.maximum, [row(v, top_row) for v in values])
            scale = [jnp.exp(row(v, top_row) - top) for v in values]
            out_ref[top_row : top_row + 1, :] = top
            for i in sums:
                out_ref[i : i + 1, :] = sum(c * row(v, i) for c, v in zip(scale, values))
        out_ref[5:6, :] = sum(row(v, 5) for v in values)
        out_ref[6:8, :] = values[0][6:8, :]

    return call(kernel, jax.ShapeDtypeStruct(stats[0].shape, F32), *stats)


def merge_all(stats):
    def kernel(in_ref, out_ref):
        for top_row, sums in ((0, (1, 2)), (3, (4,))):
            tops = in_ref[:, top_row, :]
            top = jnp.max(tops, axis=0, keepdims=True)
            scale = jnp.exp(tops - top)
            out_ref[top_row : top_row + 1, :] = top
            for i in sums:
                out_ref[i : i + 1, :] = jnp.sum(scale * in_ref[:, i, :], axis=0, keepdims=True)
        out_ref[5:6, :] = jnp.sum(in_ref[:, 5, :], axis=0, keepdims=True)
        out_ref[6:8, :] = jnp.zeros((2, in_ref.shape[2]), F32)

    return call(kernel, jax.ShapeDtypeStruct(stats.shape[1:], F32), stats)


def hidden_part(head, teacher, student, stats, targets, loss_grad, ids):
    width, depth = head.shape
    tokens = teacher.shape[1]
    half = tokens // 2
    block = 1024

    def kernel(ids_ref, w_ref, tl_ref, sl_ref, st_ref, t_ref, g_ref, own_ref, other_ref, grad):
        st = st_ref[...]
        t_probs = jnp.exp(tl_ref[...] - st[0:1, :]) / st[1:2, :]
        s_probs = jnp.exp(sl_ref[...] - st[3:4, :]) / st[4:5, :]
        hit = hits(ids_ref, t_ref, t_probs.shape)
        value = g_ref[...] * (2.0 * s_probs - t_probs - hit.astype(F32))
        first = ids_ref[0] == 0
        low, high = value[:, :half].T, value[:, half:].T
        grad[0:half, :] = jnp.where(first, low, high).astype(BF16)
        grad[half:tokens, :] = jnp.where(first, high, low).astype(BF16)
        for start in range(0, depth, block):
            cols = slice(start, start + block)
            out = jnp.dot(grad[...], w_ref[:, cols], preferred_element_type=F32)
            own_ref[:, cols] = out[:half]
            other_ref[:, cols] = out[half:].astype(BF16)

    return call(
        kernel,
        [jax.ShapeDtypeStruct((half, depth), F32), jax.ShapeDtypeStruct((half, depth), BF16)],
        ids,
        head,
        teacher,
        student,
        stats,
        targets,
        loss_grad,
        in_specs=[SMEM] + [VMEM] * 6,
        scratch=[pltpu.VMEM((tokens, width), BF16)],
    )


def body(teacher_rows, student_rows, teacher_head, student_head, targets, loss_grad):
    t_head = jnp.transpose(teacher_head, (2, 1, 0))
    s_head = jnp.transpose(student_head, (1, 0))
    width = s_head.shape[0]
    grp, vocab, seq = lax.axis_index("grp"), lax.axis_index("vocab"), lax.axis_index("seq")
    shard = (grp * lax.axis_size("vocab") + vocab) * lax.axis_size("seq") + seq
    ids = jnp.stack([grp, seq, (vocab // 4) % 4, vocab % 4, shard * width]).astype(jnp.int32)
    lower = vocab < 16
    targets2, loss_grad2 = targets.reshape(1, -1), loss_grad.reshape(1, -1)

    def pair(a):
        b = swap_xhi(a)
        return jnp.where(lower, jnp.stack([a, b]), jnp.stack([b, a]))

    after = lax.optimization_barrier
    a = jnp.broadcast_to(teacher_rows[None], (32,) + teacher_rows.shape)
    a = lax.all_to_all(a, "vocab", 0, 0, tiled=True).reshape(-1, teacher_rows.shape[1])
    planes = [[x * 16 + i for i in range(16)] for x in range(2)]
    b = pair(student_rows)
    b = jnp.broadcast_to(b[None], (16,) + b.shape)
    a, b = after((a, b))
    b = lax.all_to_all(b, "vocab", 0, 0, axis_index_groups=planes, tiled=True)

    def send(first, count):
        own, other = teacher_part(t_head, a, ids, False, first, count)
        return own, swap_core(other)

    own0, got0 = send(0, 4)
    a, own0 = after((a, own0))
    own1, other1 = teacher_part(t_head, a, ids, False, 4, 2)
    a, own1, other1, sum0 = after((a, own1, other1, own0 + got0))
    near0 = swap_seq(sum0)
    sum1 = own1 + swap_core(other1)
    mine, other = teacher_part(t_head, a, ids, True, 0, BLOCKS)
    mine, other, b, sum1, near0 = after((mine, other, b, sum1, near0))
    near1 = swap_seq(sum1)
    core = swap_core(other)
    b = place(b)
    student = student_product(s_head, b, swap_core(b), ids)
    near = [near0, near1]
    teacher, stats = local_stats(mine, core, near, student, targets2, ids)
    stats = merge([stats, swap_core(stats)])
    stats = jnp.broadcast_to(stats[None], (64,) + stats.shape)
    stats = merge_all(lax.all_to_all(stats, ("vocab", "seq"), 0, 0, tiled=True))

    own, other = hidden_part(s_head, teacher, student, stats, targets2, loss_grad2, ids)
    part = (own + swap_core(other).astype(F32)).astype(BF16)
    part = part.reshape(64, 2, -1)
    part = lax.all_to_all(part, ("vocab", "seq"), 0, 0, tiled=True)
    hidden = jnp.sum(part.astype(F32), axis=0).astype(BF16)

    t_norm = stats[0] + jnp.log(stats[1])
    s_norm = stats[3] + jnp.log(stats[4])
    token_loss = stats[2] / stats[1] - t_norm + 2.0 * s_norm - stats[5]
    return hidden, token_loss


def solution(mesh):
    return jax.shard_map(
        body,
        mesh=mesh,
        in_specs=(
            P("vocab", ("grp", "seq")),
            P(("grp", "vocab"), None),
            P(("grp", "seq"), None, "vocab"),
            P(None, ("grp", "vocab", "seq")),
            P(),
            P(),
        ),
        out_specs=(P(("grp", "vocab", "seq"), None), P()),
        check_vma=False,
    )
```

```python
import functools

import jax
import jax.numpy as jnp
from jax import lax
from jax.experimental import pallas as pl
from jax.experimental.pallas import tpu as pltpu
from jax.sharding import PartitionSpec as P

F32 = jnp.float32
BF16 = jnp.bfloat16
BLOCKS = 6
TINY = pl.CostEstimate(flops=1000, bytes_accessed=1000, transcendentals=0)
VMEM = pl.BlockSpec(memory_space=pltpu.VMEM)
SMEM = pl.BlockSpec(memory_space=pltpu.SMEM)


def params(mib=20):
    return pltpu.CompilerParams(vmem_limit_bytes=mib * 1024 * 1024)


def call(kernel, out_shape, *args, in_specs=None, scratch=(), mib=20):
    return pl.pallas_call(
        kernel,
        out_shape=out_shape,
        in_specs=in_specs or [VMEM] * len(args),
        out_specs=jax.tree.map(lambda _: VMEM, out_shape),
        scratch_shapes=scratch,
        compiler_params=params(mib),
        cost_estimate=TINY,
    )(*args)


def swap_xhi(a):
    return lax.ppermute(a, "vocab", [(i, i ^ 16) for i in range(32)])


def swap_core(a):
    return lax.ppermute(a, "grp", [(0, 1), (1, 0)])


def swap_seq(a):
    return lax.ppermute(a, "seq", [(0, 1), (1, 0)])


def spread_rows(rows, copies):
    def kernel(in_ref, out_ref):
        for i in range(copies):
            out_ref[i] = in_ref[...]

    return call(kernel, jax.ShapeDtypeStruct((copies,) + rows.shape, rows.dtype), rows)


def place(a):
    n, two, m, w = a.shape

    def kernel(in_ref, out_ref):
        for h in range(two):
            out_ref[h * n * m : (h + 1) * n * m, :] = in_ref[:, h].reshape(n * m, w)

    return call(kernel, jax.ShapeDtypeStruct((two * n * m, w), BF16), a)


def teacher_part(head, rows, ids, mine, first, count):
    width, _, depth = head.shape
    step = width // (2 * BLOCKS)
    tokens = rows.shape[0]
    padded = -(-step // 8) * 8
    pair = 2

    def place(i, ids_ref):
        part = ids_ref[1] if mine else 1 - ids_ref[1]
        return ((part * BLOCKS + first) // pair + i, 0, 0)

    def kernel(ids_ref, w_ref, x_ref, own_ref, other_ref, acc):
        g = ids_ref[0]
        w = w_ref[...].reshape(2 * pair * step, depth)
        out = lax.dot_general(w, x_ref[...], (((1,), (1,)), ((), ())), preferred_element_type=F32)
        for lane in range(tokens // 128):
            cols = slice(lane * 128, lane * 128 + 128)
            acc[lane, 0 : 2 * pair * step, :] = out[:, cols]
            for i in range(pair):
                to = slice(i * padded, i * padded + step)
                start = i * 2 * step
                own_ref[to, cols] = acc[lane, pl.ds(start + g, step, stride=2), :]
                other_ref[to, cols] = acc[lane, pl.ds(start + 1 - g, step, stride=2), :]

    out = jax.ShapeDtypeStruct((count * padded, tokens), F32)
    block = pl.BlockSpec((pair * padded, tokens), lambda i, r: (i, 0))
    return pl.pallas_call(
        kernel,
        grid_spec=pltpu.PrefetchScalarGridSpec(
            num_scalar_prefetch=1,
            grid=(count // pair,),
            in_specs=[
                pl.BlockSpec((pair * step, 2, depth), place),
                pl.BlockSpec((tokens, depth), lambda i, r: (0, 0)),
            ],
            out_specs=[block, block],
            scratch_shapes=[pltpu.VMEM((tokens // 128, 2 * pair * step + 20, 128), F32)],
        ),
        out_shape=[out, out],
        compiler_params=params(50),
        cost_estimate=TINY,
    )(ids, head, rows)


def student_product(head, own, other, ids):
    width, depth = head.shape
    half = own.shape[0]
    block = 256

    def kernel(ids_ref, w_ref, own_ref, other_ref, out_ref, xs):
        g = ids_ref[0]
        xs[pl.ds(pl.multiple_of(g * half, half), half), :] = own_ref[...]
        xs[pl.ds(pl.multiple_of((1 - g) * half, half), half), :] = other_ref[...]
        for start in range(0, width, block):
            rows = slice(start, min(start + block, width))
            out_ref[rows, :] = lax.dot_general(
                w_ref[rows, :], xs[...], (((1,), (1,)), ((), ())), preferred_element_type=F32
            )

    return call(
        kernel,
        jax.ShapeDtypeStruct((width, 2 * half), F32),
        ids,
        head,
        own,
        other,
        in_specs=[SMEM, VMEM, VMEM, VMEM],
        scratch=[pltpu.VMEM((2 * half, depth), BF16)],
    )


def hits(ids_ref, targets_ref, shape):
    columns = ids_ref[4] + lax.broadcasted_iota(jnp.int32, shape, 0)
    return columns == targets_ref[...]


def local_stats(mine, core, near, student, targets, ids):
    width, tokens = student.shape
    step = width // BLOCKS
    padded = -(-step // 8) * 8

    def kernel(ids_ref, mine_ref, core_ref, *refs):
        near_refs = refs[: len(near)]
        s_ref, t_ref, tl_ref, out_ref = refs[len(near) :]
        b = 0
        for ref in near_refs:
            for i in range(ref.shape[0] // padded):
                here = slice(b * padded, b * padded + step)
                there = slice(i * padded, i * padded + step)
                own = mine_ref[here, :] + core_ref[here, :]
                tl_ref[b * step : (b + 1) * step, :] = own + ref[there, :]
                b += 1
        t, s = tl_ref[...], s_ref[...]
        t_top = jnp.max(t, axis=0, keepdims=True)
        s_top = jnp.max(s, axis=0, keepdims=True)
        e = jnp.exp(t - t_top)
        out_ref[0:1, :] = t_top
        out_ref[1:2, :] = jnp.sum(e, axis=0, keepdims=True)
        out_ref[2:3, :] = jnp.sum(e * (t - s), axis=0, keepdims=True)
        out_ref[3:4, :] = s_top
        out_ref[4:5, :] = jnp.sum(jnp.exp(s - s_top), axis=0, keepdims=True)
        hit = hits(ids_ref, t_ref, s.shape)
        out_ref[5:6, :] = jnp.sum(jnp.where(hit, s, jnp.zeros_like(s)), axis=0, keepdims=True)
        out_ref[6:8, :] = jnp.zeros((2, tokens), F32)

    return call(
        kernel,
        [jax.ShapeDtypeStruct((width, tokens), F32), jax.ShapeDtypeStruct((8, tokens), F32)],
        ids,
        mine,
        core,
        *near,
        student,
        targets,
        in_specs=[SMEM] + [VMEM] * (4 + len(near)),
    )


def merge(stats):
    def kernel(*refs):
        out_ref = refs[-1]
        values = [r[...] for r in refs[:-1]]

        def row(v, i):
            return v[i : i + 1, :]

        for top_row, sums in ((0, (1, 2)), (3, (4,))):
            top = functools.reduce(jnp.maximum, [row(v, top_row) for v in values])
            scale = [jnp.exp(row(v, top_row) - top) for v in values]
            out_ref[top_row : top_row + 1, :] = top
            for i in sums:
                out_ref[i : i + 1, :] = sum(c * row(v, i) for c, v in zip(scale, values))
        out_ref[5:6, :] = sum(row(v, 5) for v in values)
        out_ref[6:8, :] = values[0][6:8, :]

    return call(kernel, jax.ShapeDtypeStruct(stats[0].shape, F32), *stats)


def merge_all(stats):
    def kernel(in_ref, out_ref):
        for top_row, sums in ((0, (1, 2)), (3, (4,))):
            tops = in_ref[:, top_row, :]
            top = jnp.max(tops, axis=0, keepdims=True)
            scale = jnp.exp(tops - top)
            out_ref[top_row : top_row + 1, :] = top
            for i in sums:
                out_ref[i : i + 1, :] = jnp.sum(scale * in_ref[:, i, :], axis=0, keepdims=True)
        out_ref[5:6, :] = jnp.sum(in_ref[:, 5, :], axis=0, keepdims=True)
        out_ref[6:8, :] = jnp.zeros((2, in_ref.shape[2]), F32)

    return call(kernel, jax.ShapeDtypeStruct(stats.shape[1:], F32), stats)


def hidden_part(head, teacher, student, stats, targets, loss_grad, ids):
    width, depth = head.shape
    tokens = teacher.shape[1]
    half = tokens // 2
    block = 1024

    def kernel(ids_ref, w_ref, tl_ref, sl_ref, st_ref, t_ref, g_ref, own_ref, other_ref, grad):
        st = st_ref[...]
        t_probs = jnp.exp(tl_ref[...] - st[0:1, :]) / st[1:2, :]
        s_probs = jnp.exp(sl_ref[...] - st[3:4, :]) / st[4:5, :]
        hit = hits(ids_ref, t_ref, t_probs.shape)
        value = g_ref[...] * (2.0 * s_probs - t_probs - hit.astype(F32))
        first = ids_ref[0] == 0
        low, high = value[:, :half].T, value[:, half:].T
        grad[0:half, :] = jnp.where(first, low, high).astype(BF16)
        grad[half:tokens, :] = jnp.where(first, high, low).astype(BF16)
        for start in range(0, depth, block):
            cols = slice(start, start + block)
            out = jnp.dot(grad[...], w_ref[:, cols], preferred_element_type=F32)
            own_ref[:, cols] = out[:half]
            other_ref[:, cols] = out[half:].astype(BF16)

    return call(
        kernel,
        [jax.ShapeDtypeStruct((half, depth), F32), jax.ShapeDtypeStruct((half, depth), BF16)],
        ids,
        head,
        teacher,
        student,
        stats,
        targets,
        loss_grad,
        in_specs=[SMEM] + [VMEM] * 6,
        scratch=[pltpu.VMEM((tokens, width), BF16)],
    )


def add_parts(own, other, blocks):
    tokens, depth = own.shape

    def kernel(own_ref, other_ref, out_ref):
        total = own_ref[...] + other_ref[...].astype(F32)
        out_ref[...] = total.reshape(out_ref.shape).astype(BF16)

    return call(kernel, jax.ShapeDtypeStruct((blocks, tokens // blocks, depth), BF16), own, other)


def sum_parts(parts):
    def kernel(in_ref, out_ref):
        total = in_ref[0].astype(F32)
        for i in range(1, in_ref.shape[0]):
            total += in_ref[i].astype(F32)
        out_ref[...] = total.astype(BF16)

    return call(kernel, jax.ShapeDtypeStruct(parts.shape[1:], BF16), parts)


def body(teacher_rows, student_rows, teacher_head, student_head, targets, loss_grad):
    t_head = jnp.transpose(teacher_head, (2, 1, 0))
    s_head = jnp.transpose(student_head, (1, 0))
    width = s_head.shape[0]
    grp, vocab, seq = lax.axis_index("grp"), lax.axis_index("vocab"), lax.axis_index("seq")
    shard = (grp * lax.axis_size("vocab") + vocab) * lax.axis_size("seq") + seq
    ids = jnp.stack([grp, seq, (vocab // 4) % 4, vocab % 4, shard * width]).astype(jnp.int32)
    targets2, loss_grad2 = targets.reshape(1, -1), loss_grad.reshape(1, -1)

    after = lax.optimization_barrier

    near_b = swap_xhi(student_rows)
    pair = [jnp.where(vocab < 16, p, q) for p, q in ((student_rows, near_b), (near_b, student_rows))]
    b = spread_rows(jnp.stack(pair), 16)
    a = spread_rows(teacher_rows, lax.axis_size("vocab"))
    a = lax.all_to_all(a, "vocab", 0, 0, tiled=True).reshape(-1, teacher_rows.shape[1])
    a, b = after((a, b))
    planes = [[x * 16 + i for i in range(16)] for x in range(2)]
    b = lax.all_to_all(b, "vocab", 0, 0, axis_index_groups=planes, tiled=True)

    own0, other0 = teacher_part(t_head, a, ids, False, 0, 2)
    a, sum0 = after((a, own0 + swap_core(other0)))
    near0 = swap_seq(sum0)
    own1, other1 = teacher_part(t_head, a, ids, False, 2, 4)
    a, own1, other1, near0, b = after((a, own1, other1, near0, b))
    got1 = swap_core(other1)
    b = place(b)
    b_other = swap_core(b)
    half = sum0.shape[0]
    sum1, sum2 = own1[:half] + got1[:half], own1[half:] + got1[half:]
    a, b, b_other, sum1, sum2 = after((a, b, b_other, sum1, sum2))
    near1 = swap_seq(sum1)
    mine, other = teacher_part(t_head, a, ids, True, 0, BLOCKS)
    mine, other, b, b_other, sum2, near1 = after((mine, other, b, b_other, sum2, near1))
    near2 = swap_seq(sum2)
    core = swap_core(other)
    student = student_product(s_head, b, b_other, ids)
    near = [near0, near1, near2]
    teacher, stats = local_stats(mine, core, near, student, targets2, ids)
    stats = merge([stats, swap_core(stats)])
    stats = jnp.broadcast_to(stats[None], (64,) + stats.shape)
    stats = merge_all(lax.all_to_all(stats, ("vocab", "seq"), 0, 0, tiled=True))

    own, other = hidden_part(s_head, teacher, student, stats, targets2, loss_grad2, ids)
    part = add_parts(own, swap_core(other), 64)
    part = lax.all_to_all(part, ("vocab", "seq"), 0, 0, tiled=True)
    hidden = sum_parts(part)

    t_norm = stats[0] + jnp.log(stats[1])
    s_norm = stats[3] + jnp.log(stats[4])
    token_loss = stats[2] / stats[1] - t_norm + 2.0 * s_norm - stats[5]
    return hidden, token_loss


def solution(mesh):
    return jax.shard_map(
        body,
        mesh=mesh,
        in_specs=(
            P("vocab", ("grp", "seq")),
            P(("grp", "vocab"), None),
            P(("grp", "seq"), None, "vocab"),
            P(None, ("grp", "vocab", "seq")),
            P(),
            P(),
        ),
        out_specs=(P(("grp", "vocab", "seq"), None), P()),
        check_vma=False,
    )
```

```python
import functools

import jax
import jax.numpy as jnp
from jax import lax
from jax.experimental import pallas as pl
from jax.experimental.pallas import tpu as pltpu
from jax.sharding import PartitionSpec as P

F32 = jnp.float32
BF16 = jnp.bfloat16
BLOCKS = 6
TINY = pl.CostEstimate(flops=1000, bytes_accessed=1000, transcendentals=0)
VMEM = pl.BlockSpec(memory_space=pltpu.VMEM)
SMEM = pl.BlockSpec(memory_space=pltpu.SMEM)


def params(mib=20):
    return pltpu.CompilerParams(vmem_limit_bytes=mib * 1024 * 1024)


def call(kernel, out_shape, *args, in_specs=None, scratch=(), mib=20):
    return pl.pallas_call(
        kernel,
        out_shape=out_shape,
        in_specs=in_specs or [VMEM] * len(args),
        out_specs=jax.tree.map(lambda _: VMEM, out_shape),
        scratch_shapes=scratch,
        compiler_params=params(mib),
        cost_estimate=TINY,
    )(*args)


def swap_xhi(a):
    return lax.ppermute(a, "vocab", [(i, i ^ 16) for i in range(32)])


def swap_core(a):
    return lax.ppermute(a, "grp", [(0, 1), (1, 0)])


def swap_seq(a):
    return lax.ppermute(a, "seq", [(0, 1), (1, 0)])


def spread_rows(rows, copies):
    def kernel(in_ref, out_ref):
        for i in range(copies):
            out_ref[i] = in_ref[...]

    return call(kernel, jax.ShapeDtypeStruct((copies,) + rows.shape, rows.dtype), rows)


def place(a):
    n, two, m, w = a.shape

    def kernel(in_ref, out_ref):
        for h in range(two):
            out_ref[h * n * m : (h + 1) * n * m, :] = in_ref[:, h].reshape(n * m, w)

    return call(kernel, jax.ShapeDtypeStruct((two * n * m, w), BF16), a)


def teacher_part(head, rows, ids, mine, first, count):
    width, _, depth = head.shape
    step = width // (2 * BLOCKS)
    tokens = rows.shape[0]
    padded = -(-step // 8) * 8
    pair = min(count, 3)

    def place(i, ids_ref):
        part = ids_ref[1] if mine else 1 - ids_ref[1]
        return ((part * BLOCKS + first) // pair + i, 0, 0)

    def kernel(ids_ref, w_ref, x_ref, own_ref, other_ref, acc):
        g = ids_ref[0]
        w = w_ref[...].reshape(2 * pair * step, depth)
        out = lax.dot_general(w, x_ref[...], (((1,), (1,)), ((), ())), preferred_element_type=F32)
        for lane in range(tokens // 128):
            cols = slice(lane * 128, lane * 128 + 128)
            acc[lane, 0 : 2 * pair * step, :] = out[:, cols]
            for i in range(pair):
                to = slice(i * padded, i * padded + step)
                start = i * 2 * step
                own_ref[to, cols] = acc[lane, pl.ds(start + g, step, stride=2), :]
                other_ref[to, cols] = acc[lane, pl.ds(start + 1 - g, step, stride=2), :]

    out = jax.ShapeDtypeStruct((count * padded, tokens), F32)
    block = pl.BlockSpec((pair * padded, tokens), lambda i, r: (i, 0))
    return pl.pallas_call(
        kernel,
        grid_spec=pltpu.PrefetchScalarGridSpec(
            num_scalar_prefetch=1,
            grid=(count // pair,),
            in_specs=[
                pl.BlockSpec((pair * step, 2, depth), place),
                pl.BlockSpec((tokens, depth), lambda i, r: (0, 0)),
            ],
            out_specs=[block, block],
            scratch_shapes=[pltpu.VMEM((tokens // 128, 2 * pair * step + 20, 128), F32)],
        ),
        out_shape=[out, out],
        compiler_params=params(50),
        cost_estimate=TINY,
    )(ids, head, rows)


def student_product(head, own, other, ids):
    width, depth = head.shape
    half = own.shape[0]
    block = 256

    def kernel(ids_ref, w_ref, own_ref, other_ref, out_ref, xs):
        g = ids_ref[0]
        xs[pl.ds(pl.multiple_of(g * half, half), half), :] = own_ref[...]
        xs[pl.ds(pl.multiple_of((1 - g) * half, half), half), :] = other_ref[...]
        for start in range(0, width, block):
            rows = slice(start, min(start + block, width))
            out_ref[rows, :] = lax.dot_general(
                w_ref[rows, :], xs[...], (((1,), (1,)), ((), ())), preferred_element_type=F32
            )

    return call(
        kernel,
        jax.ShapeDtypeStruct((width, 2 * half), F32),
        ids,
        head,
        own,
        other,
        in_specs=[SMEM, VMEM, VMEM, VMEM],
        scratch=[pltpu.VMEM((2 * half, depth), BF16)],
    )


def hits(ids_ref, targets_ref, shape):
    columns = ids_ref[4] + lax.broadcasted_iota(jnp.int32, shape, 0)
    return columns == targets_ref[...]


def local_stats(mine, core, near, student, targets, ids):
    width, tokens = student.shape
    step = width // BLOCKS
    padded = -(-step // 8) * 8

    def kernel(ids_ref, mine_ref, core_ref, *refs):
        near_refs = refs[: len(near)]
        s_ref, t_ref, te_ref, se_ref, out_ref = refs[len(near) :]
        b = 0
        for ref in near_refs:
            for i in range(ref.shape[0] // padded):
                here = slice(b * padded, b * padded + step)
                there = slice(i * padded, i * padded + step)
                own = mine_ref[here, :] + core_ref[here, :]
                te_ref[b * step : (b + 1) * step, :] = own + ref[there, :]
                b += 1
        t, s = te_ref[...], s_ref[...]
        t_top = jnp.max(t, axis=0, keepdims=True)
        s_top = jnp.max(s, axis=0, keepdims=True)
        e = jnp.exp(t - t_top)
        te_ref[...] = e
        out_ref[0:1, :] = t_top
        out_ref[1:2, :] = jnp.sum(e, axis=0, keepdims=True)
        out_ref[2:3, :] = jnp.sum(e * (t - s), axis=0, keepdims=True)
        out_ref[3:4, :] = s_top
        e = jnp.exp(s - s_top)
        se_ref[...] = e
        out_ref[4:5, :] = jnp.sum(e, axis=0, keepdims=True)
        hit = hits(ids_ref, t_ref, s.shape)
        out_ref[5:6, :] = jnp.sum(jnp.where(hit, s, jnp.zeros_like(s)), axis=0, keepdims=True)
        out_ref[6:8, :] = jnp.zeros((2, tokens), F32)

    return call(
        kernel,
        [jax.ShapeDtypeStruct((width, tokens), F32)] * 2 + [jax.ShapeDtypeStruct((8, tokens), F32)],
        ids,
        mine,
        core,
        *near,
        student,
        targets,
        in_specs=[SMEM] + [VMEM] * (4 + len(near)),
    )


def merge(stats):
    def kernel(*refs):
        out_ref = refs[-1]
        values = [r[...] for r in refs[:-1]]

        def row(v, i):
            return v[i : i + 1, :]

        for top_row, sums in ((0, (1, 2)), (3, (4,))):
            top = functools.reduce(jnp.maximum, [row(v, top_row) for v in values])
            scale = [jnp.exp(row(v, top_row) - top) for v in values]
            out_ref[top_row : top_row + 1, :] = top
            for i in sums:
                out_ref[i : i + 1, :] = sum(c * row(v, i) for c, v in zip(scale, values))
        out_ref[5:6, :] = sum(row(v, 5) for v in values)
        out_ref[6:8, :] = values[0][6:8, :]

    return call(kernel, jax.ShapeDtypeStruct(stats[0].shape, F32), *stats)


def merge_all(stats):
    def kernel(in_ref, out_ref):
        for top_row, sums in ((0, (1, 2)), (3, (4,))):
            tops = in_ref[:, top_row, :]
            top = jnp.max(tops, axis=0, keepdims=True)
            scale = jnp.exp(tops - top)
            out_ref[top_row : top_row + 1, :] = top
            for i in sums:
                out_ref[i : i + 1, :] = jnp.sum(scale * in_ref[:, i, :], axis=0, keepdims=True)
        out_ref[5:6, :] = jnp.sum(in_ref[:, 5, :], axis=0, keepdims=True)
        out_ref[6:8, :] = jnp.zeros((2, in_ref.shape[2]), F32)

    return call(kernel, jax.ShapeDtypeStruct(stats.shape[1:], F32), stats)


def hidden_part(head, teacher, student, here, stats, targets, loss_grad, ids):
    width, depth = head.shape
    tokens = teacher.shape[1]
    half = tokens // 2
    block = 1024

    def kernel(
        ids_ref, w_ref, te_ref, se_ref, here_ref, st_ref, t_ref, g_ref, own_ref, other_ref, grad
    ):
        st, here = st_ref[...], here_ref[...]
        t_probs = te_ref[...] * (jnp.exp(here[0:1, :] - st[0:1, :]) / st[1:2, :])
        s_probs = se_ref[...] * (jnp.exp(here[3:4, :] - st[3:4, :]) / st[4:5, :])
        hit = hits(ids_ref, t_ref, t_probs.shape)
        value = g_ref[...] * (2.0 * s_probs - t_probs - hit.astype(F32))
        first = ids_ref[0] == 0
        low, high = value[:, :half].T, value[:, half:].T
        grad[0:half, :] = jnp.where(first, low, high).astype(BF16)
        grad[half:tokens, :] = jnp.where(first, high, low).astype(BF16)
        for start in range(0, depth, block):
            cols = slice(start, start + block)
            out = jnp.dot(grad[...], w_ref[:, cols], preferred_element_type=F32)
            own_ref[:, cols] = out[:half]
            other_ref[:, cols] = out[half:].astype(BF16)

    return call(
        kernel,
        [jax.ShapeDtypeStruct((half, depth), F32), jax.ShapeDtypeStruct((half, depth), BF16)],
        ids,
        head,
        teacher,
        student,
        here,
        stats,
        targets,
        loss_grad,
        in_specs=[SMEM] + [VMEM] * 7,
        scratch=[pltpu.VMEM((tokens, width), BF16)],
    )


def add_parts(own, other, blocks):
    tokens, depth = own.shape

    def kernel(own_ref, other_ref, out_ref):
        total = own_ref[...] + other_ref[...].astype(F32)
        out_ref[...] = total.reshape(out_ref.shape).astype(BF16)

    return call(kernel, jax.ShapeDtypeStruct((blocks, tokens // blocks, depth), BF16), own, other)


def sum_parts(parts):
    def kernel(in_ref, out_ref):
        total = in_ref[0].astype(F32)
        for i in range(1, in_ref.shape[0]):
            total += in_ref[i].astype(F32)
        out_ref[...] = total.astype(BF16)

    return call(kernel, jax.ShapeDtypeStruct(parts.shape[1:], BF16), parts)


def body(teacher_rows, student_rows, teacher_head, student_head, targets, loss_grad):
    t_head = jnp.transpose(teacher_head, (2, 1, 0))
    s_head = jnp.transpose(student_head, (1, 0))
    width = s_head.shape[0]
    grp, vocab, seq = lax.axis_index("grp"), lax.axis_index("vocab"), lax.axis_index("seq")
    shard = (grp * lax.axis_size("vocab") + vocab) * lax.axis_size("seq") + seq
    ids = jnp.stack([grp, seq, (vocab // 4) % 4, vocab % 4, shard * width]).astype(jnp.int32)
    targets2, loss_grad2 = targets.reshape(1, -1), loss_grad.reshape(1, -1)

    after = lax.optimization_barrier

    near_b = swap_xhi(student_rows)
    pair = [jnp.where(vocab < 16, p, q) for p, q in ((student_rows, near_b), (near_b, student_rows))]
    b = spread_rows(jnp.stack(pair), 16)
    a = spread_rows(teacher_rows, lax.axis_size("vocab"))
    a = lax.all_to_all(a, "vocab", 0, 0, tiled=True).reshape(-1, teacher_rows.shape[1])
    a, b = after((a, b))
    planes = [[x * 16 + i for i in range(16)] for x in range(2)]
    b = lax.all_to_all(b, "vocab", 0, 0, axis_index_groups=planes, tiled=True)

    own0, other0 = teacher_part(t_head, a, ids, False, 0, 2)
    got0 = swap_core(other0)
    a, own0 = after((a, own0))
    own1, other1 = teacher_part(t_head, a, ids, False, 2, 2)
    a, own1, other1, sum0 = after((a, own1, other1, own0 + got0))
    near0 = swap_seq(sum0)
    sum1 = own1 + swap_core(other1)
    own2, other2 = teacher_part(t_head, a, ids, False, 4, 2)
    a, own2, other2, sum1, near0, b = after((a, own2, other2, sum1, near0, b))
    b = place(b)
    a, own2, other2, sum1, b = after((a, own2, other2, sum1, b))
    near1 = swap_seq(sum1)
    sum2 = own2 + swap_core(other2)
    b_other = swap_core(b)
    mine, other = teacher_part(t_head, a, ids, True, 0, BLOCKS)
    mine, other, b, b_other, sum2, near1 = after((mine, other, b, b_other, sum2, near1))
    near2 = swap_seq(sum2)
    core = swap_core(other)
    student = student_product(s_head, b, b_other, ids)
    near = [near0, near1, near2]
    teacher, student, here = local_stats(mine, core, near, student, targets2, ids)
    stats = merge([here, swap_core(here)])
    stats = spread_rows(stats, 64)
    stats = merge_all(lax.all_to_all(stats, ("vocab", "seq"), 0, 0, tiled=True))

    own, other = hidden_part(s_head, teacher, student, here, stats, targets2, loss_grad2, ids)
    part = add_parts(own, swap_core(other), 64)
    part = lax.all_to_all(part, ("vocab", "seq"), 0, 0, tiled=True)
    hidden = sum_parts(part)

    t_norm = stats[0] + jnp.log(stats[1])
    s_norm = stats[3] + jnp.log(stats[4])
    token_loss = stats[2] / stats[1] - t_norm + 2.0 * s_norm - stats[5]
    return hidden, token_loss


def solution(mesh):
    return jax.shard_map(
        body,
        mesh=mesh,
        in_specs=(
            P("vocab", ("grp", "seq")),
            P(("grp", "vocab"), None),
            P(("grp", "seq"), None, "vocab"),
            P(None, ("grp", "vocab", "seq")),
            P(),
            P(),
        ),
        out_specs=(P(("grp", "vocab", "seq"), None), P()),
        check_vma=False,
    )
```

```python
import functools

import jax
import jax.numpy as jnp
from jax import lax
from jax.experimental import pallas as pl
from jax.experimental.pallas import tpu as pltpu
from jax.sharding import PartitionSpec as P

F32 = jnp.float32
BF16 = jnp.bfloat16
BLOCKS = 6
TINY = pl.CostEstimate(flops=1000, bytes_accessed=1000, transcendentals=0)
VMEM = pl.BlockSpec(memory_space=pltpu.VMEM)
SMEM = pl.BlockSpec(memory_space=pltpu.SMEM)


def params(mib=20):
    return pltpu.CompilerParams(vmem_limit_bytes=mib * 1024 * 1024)


def call(kernel, out_shape, *args, in_specs=None, scratch=(), mib=20):
    return pl.pallas_call(
        kernel,
        out_shape=out_shape,
        in_specs=in_specs or [VMEM] * len(args),
        out_specs=jax.tree.map(lambda _: VMEM, out_shape),
        scratch_shapes=scratch,
        compiler_params=params(mib),
        cost_estimate=TINY,
    )(*args)


def swap_xhi(a):
    return lax.ppermute(a, "vocab", [(i, i ^ 16) for i in range(32)])


def swap_core(a):
    return lax.ppermute(a, "grp", [(0, 1), (1, 0)])


def swap_seq(a):
    return lax.ppermute(a, "seq", [(0, 1), (1, 0)])


def spread_rows(rows, copies):
    def kernel(in_ref, out_ref):
        for i in range(copies):
            out_ref[i] = in_ref[...]

    return call(kernel, jax.ShapeDtypeStruct((copies,) + rows.shape, rows.dtype), rows)


def place(a):
    n, two, m, w = a.shape

    def kernel(in_ref, out_ref):
        for h in range(two):
            out_ref[h * n * m : (h + 1) * n * m, :] = in_ref[:, h].reshape(n * m, w)

    return call(kernel, jax.ShapeDtypeStruct((two * n * m, w), BF16), a)


def teacher_part(head, rows, ids, mine, first, count):
    width, _, depth = head.shape
    step = width // (2 * BLOCKS)
    tokens = rows.shape[0]
    padded = -(-step // 8) * 8
    pair = min(count, 3)

    def place(i, ids_ref):
        part = ids_ref[1] if mine else 1 - ids_ref[1]
        return ((part * BLOCKS + first) // pair + i, 0, 0)

    def kernel(ids_ref, w_ref, x_ref, own_ref, other_ref, acc):
        g = ids_ref[0]
        w = w_ref[...].reshape(2 * pair * step, depth)
        out = lax.dot_general(w, x_ref[...], (((1,), (1,)), ((), ())), preferred_element_type=F32)
        for lane in range(tokens // 128):
            cols = slice(lane * 128, lane * 128 + 128)
            acc[lane, 0 : 2 * pair * step, :] = out[:, cols]
            for i in range(pair):
                to = slice(i * padded, i * padded + step)
                start = i * 2 * step
                own_ref[to, cols] = acc[lane, pl.ds(start + g, step, stride=2), :]
                other_ref[to, cols] = acc[lane, pl.ds(start + 1 - g, step, stride=2), :]

    out = jax.ShapeDtypeStruct((count * padded, tokens), F32)
    block = pl.BlockSpec((pair * padded, tokens), lambda i, r: (i, 0))
    return pl.pallas_call(
        kernel,
        grid_spec=pltpu.PrefetchScalarGridSpec(
            num_scalar_prefetch=1,
            grid=(count // pair,),
            in_specs=[
                pl.BlockSpec((pair * step, 2, depth), place),
                pl.BlockSpec((tokens, depth), lambda i, r: (0, 0)),
            ],
            out_specs=[block, block],
            scratch_shapes=[pltpu.VMEM((tokens // 128, 2 * pair * step + 20, 128), F32)],
        ),
        out_shape=[out, out],
        compiler_params=params(50),
        cost_estimate=TINY,
    )(ids, head, rows)


def hits(ids_ref, targets_ref, shape):
    columns = ids_ref[4] + lax.broadcasted_iota(jnp.int32, shape, 0)
    return columns == targets_ref[...]


def student_product(head, own, other, targets, ids):
    width, depth = head.shape
    half = own.shape[0]
    tokens = 2 * half
    block = 256

    def kernel(ids_ref, w_ref, own_ref, other_ref, t_ref, s_ref, e_ref, out_ref, xs):
        g = ids_ref[0]
        xs[pl.ds(pl.multiple_of(g * half, half), half), :] = own_ref[...]
        xs[pl.ds(pl.multiple_of((1 - g) * half, half), half), :] = other_ref[...]
        for start in range(0, width, block):
            rows = slice(start, min(start + block, width))
            s_ref[rows, :] = lax.dot_general(
                w_ref[rows, :], xs[...], (((1,), (1,)), ((), ())), preferred_element_type=F32
            )
        s = s_ref[...]
        top = jnp.max(s, axis=0, keepdims=True)
        e = jnp.exp(s - top)
        e_ref[...] = e
        hit = hits(ids_ref, t_ref, s.shape)
        out_ref[...] = jnp.zeros_like(out_ref)
        out_ref[3:4, :] = top
        out_ref[4:5, :] = jnp.sum(e, axis=0, keepdims=True)
        out_ref[5:6, :] = jnp.sum(jnp.where(hit, s, jnp.zeros_like(s)), axis=0, keepdims=True)

    logits = jax.ShapeDtypeStruct((width, tokens), F32)
    return call(
        kernel,
        [logits, logits, jax.ShapeDtypeStruct((8, tokens), F32)],
        ids,
        head,
        own,
        other,
        targets,
        in_specs=[SMEM] + [VMEM] * 4,
        scratch=[pltpu.VMEM((tokens, depth), BF16)],
    )


def local_stats(mine, core, near, student, student_stats):
    width, tokens = student.shape
    step = width // BLOCKS
    padded = -(-step // 8) * 8

    def kernel(mine_ref, core_ref, *refs):
        near_refs = refs[: len(near)]
        s_ref, in_ref, te_ref, out_ref = refs[len(near) :]
        b = 0
        for ref in near_refs:
            for i in range(ref.shape[0] // padded):
                here = slice(b * padded, b * padded + step)
                there = slice(i * padded, i * padded + step)
                own = mine_ref[here, :] + core_ref[here, :]
                te_ref[b * step : (b + 1) * step, :] = own + ref[there, :]
                b += 1
        t = te_ref[...]
        top = jnp.max(t, axis=0, keepdims=True)
        e = jnp.exp(t - top)
        te_ref[...] = e
        out_ref[...] = in_ref[...]
        out_ref[0:1, :] = top
        out_ref[1:2, :] = jnp.sum(e, axis=0, keepdims=True)
        out_ref[2:3, :] = jnp.sum(e * (t - s_ref[...]), axis=0, keepdims=True)

    return call(
        kernel,
        [jax.ShapeDtypeStruct((width, tokens), F32), jax.ShapeDtypeStruct((8, tokens), F32)],
        mine,
        core,
        *near,
        student,
        student_stats,
    )


def merge(stats):
    def kernel(*refs):
        out_ref = refs[-1]
        values = [r[...] for r in refs[:-1]]

        def row(v, i):
            return v[i : i + 1, :]

        for top_row, sums in ((0, (1, 2)), (3, (4,))):
            top = functools.reduce(jnp.maximum, [row(v, top_row) for v in values])
            scale = [jnp.exp(row(v, top_row) - top) for v in values]
            out_ref[top_row : top_row + 1, :] = top
            for i in sums:
                out_ref[i : i + 1, :] = sum(c * row(v, i) for c, v in zip(scale, values))
        out_ref[5:6, :] = sum(row(v, 5) for v in values)
        out_ref[6:8, :] = values[0][6:8, :]

    return call(kernel, jax.ShapeDtypeStruct(stats[0].shape, F32), *stats)


def merge_all(stats):
    def kernel(in_ref, out_ref):
        for top_row, sums in ((0, (1, 2)), (3, (4,))):
            tops = in_ref[:, top_row, :]
            top = jnp.max(tops, axis=0, keepdims=True)
            scale = jnp.exp(tops - top)
            out_ref[top_row : top_row + 1, :] = top
            for i in sums:
                out_ref[i : i + 1, :] = jnp.sum(scale * in_ref[:, i, :], axis=0, keepdims=True)
        out_ref[5:6, :] = jnp.sum(in_ref[:, 5, :], axis=0, keepdims=True)
        out_ref[6:8, :] = jnp.zeros((2, in_ref.shape[2]), F32)

    return call(kernel, jax.ShapeDtypeStruct(stats.shape[1:], F32), stats)


def hidden_part(head, teacher, student, here, stats, targets, loss_grad, ids):
    width, depth = head.shape
    tokens = teacher.shape[1]
    half = tokens // 2
    block = 1024

    def kernel(
        ids_ref, w_ref, te_ref, se_ref, here_ref, st_ref, t_ref, g_ref, own_ref, other_ref, grad
    ):
        st, here = st_ref[...], here_ref[...]
        t_probs = te_ref[...] * (jnp.exp(here[0:1, :] - st[0:1, :]) / st[1:2, :])
        s_probs = se_ref[...] * (jnp.exp(here[3:4, :] - st[3:4, :]) / st[4:5, :])
        hit = hits(ids_ref, t_ref, t_probs.shape)
        value = g_ref[...] * (2.0 * s_probs - t_probs - hit.astype(F32))
        first = ids_ref[0] == 0
        low, high = value[:, :half].T, value[:, half:].T
        grad[0:half, :] = jnp.where(first, low, high).astype(BF16)
        grad[half:tokens, :] = jnp.where(first, high, low).astype(BF16)
        for start in range(0, depth, block):
            cols = slice(start, start + block)
            out = jnp.dot(grad[...], w_ref[:, cols], preferred_element_type=F32)
            own_ref[:, cols] = out[:half]
            other_ref[:, cols] = out[half:].astype(BF16)

    return call(
        kernel,
        [jax.ShapeDtypeStruct((half, depth), F32), jax.ShapeDtypeStruct((half, depth), BF16)],
        ids,
        head,
        teacher,
        student,
        here,
        stats,
        targets,
        loss_grad,
        in_specs=[SMEM] + [VMEM] * 7,
        scratch=[pltpu.VMEM((tokens, width), BF16)],
    )


def add_parts(own, other, blocks):
    tokens, depth = own.shape

    def kernel(own_ref, other_ref, out_ref):
        size = depth // 4
        for start in range(0, depth, size):
            cols = slice(start, start + size)
            total = (own_ref[:, cols] + other_ref[:, cols].astype(F32)).astype(BF16)
            out_ref[:, :, cols] = total.reshape(blocks, tokens // blocks, size)

    return call(kernel, jax.ShapeDtypeStruct((blocks, tokens // blocks, depth), BF16), own, other)


def sum_parts(parts):
    def kernel(in_ref, out_ref):
        total = in_ref[0].astype(F32)
        for i in range(1, in_ref.shape[0]):
            total += in_ref[i].astype(F32)
        out_ref[...] = total.astype(BF16)

    return call(kernel, jax.ShapeDtypeStruct(parts.shape[1:], BF16), parts)


def body(teacher_rows, student_rows, teacher_head, student_head, targets, loss_grad):
    t_head = jnp.transpose(teacher_head, (2, 1, 0))
    s_head = jnp.transpose(student_head, (1, 0))
    width = s_head.shape[0]
    grp, vocab, seq = lax.axis_index("grp"), lax.axis_index("vocab"), lax.axis_index("seq")
    shard = (grp * lax.axis_size("vocab") + vocab) * lax.axis_size("seq") + seq
    ids = jnp.stack([grp, seq, (vocab // 4) % 4, vocab % 4, shard * width]).astype(jnp.int32)
    targets2, loss_grad2 = targets.reshape(1, -1), loss_grad.reshape(1, -1)

    after = lax.optimization_barrier

    a = spread_rows(teacher_rows, lax.axis_size("vocab"))
    a, student_rows = after((a, student_rows))
    near_b = swap_xhi(student_rows)
    pair = [jnp.where(vocab < 16, p, q) for p, q in ((student_rows, near_b), (near_b, student_rows))]
    b = spread_rows(jnp.stack(pair), 16)
    a = lax.all_to_all(a, "vocab", 0, 0, tiled=True).reshape(-1, teacher_rows.shape[1])
    a, b = after((a, b))
    planes = [[x * 16 + i for i in range(16)] for x in range(2)]
    b = lax.all_to_all(b, "vocab", 0, 0, axis_index_groups=planes, tiled=True)

    own0, other0 = teacher_part(t_head, a, ids, False, 0, 2)
    got0 = swap_core(other0)
    a, own0 = after((a, own0))
    own1, other1 = teacher_part(t_head, a, ids, False, 2, 2)
    a, own1, other1, sum0 = after((a, own1, other1, own0 + got0))
    near0 = swap_seq(sum0)
    sum1 = own1 + swap_core(other1)
    own2, other2 = teacher_part(t_head, a, ids, False, 4, 2)
    a, own2, other2, sum1, near0, b = after((a, own2, other2, sum1, near0, b))
    b = place(b)
    a, own2, other2, sum1, b = after((a, own2, other2, sum1, b))
    near1 = swap_seq(sum1)
    sum2 = own2 + swap_core(other2)
    b_other = swap_core(b)
    mine, other = teacher_part(t_head, a, ids, True, 0, BLOCKS)
    mine, other, b, b_other, sum2, near1 = after((mine, other, b, b_other, sum2, near1))
    near2 = swap_seq(sum2)
    core = swap_core(other)
    logits, student, student_stats = student_product(s_head, b, b_other, targets2, ids)
    near = [near0, near1, near2]
    teacher, here = local_stats(mine, core, near, logits, student_stats)
    stats = merge([here, swap_core(here)])
    stats = spread_rows(stats, 64)
    stats = merge_all(lax.all_to_all(stats, ("vocab", "seq"), 0, 0, tiled=True))

    own, other = hidden_part(s_head, teacher, student, here, stats, targets2, loss_grad2, ids)
    part = add_parts(own, swap_core(other), 64)
    part = lax.all_to_all(part, ("vocab", "seq"), 0, 0, tiled=True)
    hidden = sum_parts(part)

    t_norm = stats[0] + jnp.log(stats[1])
    s_norm = stats[3] + jnp.log(stats[4])
    token_loss = stats[2] / stats[1] - t_norm + 2.0 * s_norm - stats[5]
    return hidden, token_loss


def solution(mesh):
    return jax.shard_map(
        body,
        mesh=mesh,
        in_specs=(
            P("vocab", ("grp", "seq")),
            P(("grp", "vocab"), None),
            P(("grp", "seq"), None, "vocab"),
            P(None, ("grp", "vocab", "seq")),
            P(),
            P(),
        ),
        out_specs=(P(("grp", "vocab", "seq"), None), P()),
        check_vma=False,
    )
```

```python
import functools

import jax
import jax.numpy as jnp
from jax import lax
from jax.experimental import pallas as pl
from jax.experimental.pallas import tpu as pltpu
from jax.sharding import PartitionSpec as P

F32 = jnp.float32
BF16 = jnp.bfloat16
BLOCKS = 6
TINY = pl.CostEstimate(flops=1000, bytes_accessed=1000, transcendentals=0)
VMEM = pl.BlockSpec(memory_space=pltpu.VMEM)
SMEM = pl.BlockSpec(memory_space=pltpu.SMEM)


def params(mib=20):
    return pltpu.CompilerParams(vmem_limit_bytes=mib * 1024 * 1024)


def call(kernel, out_shape, *args, in_specs=None, scratch=(), mib=20):
    return pl.pallas_call(
        kernel,
        out_shape=out_shape,
        in_specs=in_specs or [VMEM] * len(args),
        out_specs=jax.tree.map(lambda _: VMEM, out_shape),
        scratch_shapes=scratch,
        compiler_params=params(mib),
        cost_estimate=TINY,
    )(*args)


def swap_xhi(a):
    return lax.ppermute(a, "vocab", [(i, i ^ 16) for i in range(32)])


def swap_core(a):
    return lax.ppermute(a, "grp", [(0, 1), (1, 0)])


def swap_seq(a):
    return lax.ppermute(a, "seq", [(0, 1), (1, 0)])


def spread_rows(rows, copies):
    def kernel(in_ref, out_ref):
        for i in range(copies):
            out_ref[i] = in_ref[...]

    return call(kernel, jax.ShapeDtypeStruct((copies,) + rows.shape, rows.dtype), rows)


def place(a):
    n, two, m, w = a.shape

    def kernel(in_ref, out_ref):
        for h in range(two):
            out_ref[h * n * m : (h + 1) * n * m, :] = in_ref[:, h].reshape(n * m, w)

    return call(kernel, jax.ShapeDtypeStruct((two * n * m, w), BF16), a)


def teacher_part(head, rows, ids, mine, first, count, split=False):
    width, _, depth = head.shape
    step = width // (2 * BLOCKS)
    tokens = rows.shape[0]
    padded = -(-step // 8) * 8
    pair = 2 if split else min(count, 3)
    steps = count // pair

    def place(i, ids_ref):
        part = ids_ref[1] if mine else 1 - ids_ref[1]
        return ((part * BLOCKS + first) // pair + i, 0, 0)

    def kernel(ids_ref, w_ref, x_ref, *refs):
        acc = refs[-1]
        g = ids_ref[0]
        w = w_ref[...].reshape(2 * pair * step, depth)
        out = lax.dot_general(w, x_ref[...], (((1,), (1,)), ((), ())), preferred_element_type=F32)
        for lane in range(tokens // 128):
            acc[lane, 0 : 2 * pair * step, :] = out[:, lane * 128 : lane * 128 + 128]

        def store(own_ref, other_ref):
            for lane in range(tokens // 128):
                cols = slice(lane * 128, lane * 128 + 128)
                for i in range(pair):
                    to = slice(i * padded, i * padded + step)
                    start = i * 2 * step
                    own_ref[to, cols] = acc[lane, pl.ds(start + g, step, stride=2), :]
                    other_ref[to, cols] = acc[lane, pl.ds(start + 1 - g, step, stride=2), :]

        if split:
            for j in range(steps):
                pl.when(pl.program_id(0) == j)(
                    functools.partial(store, refs[2 * j], refs[2 * j + 1])
                )
        else:
            store(refs[0], refs[1])

    if split:
        out = jax.ShapeDtypeStruct((pair * padded, tokens), F32)
        block = pl.BlockSpec((pair * padded, tokens), lambda i, r: (0, 0))
    else:
        out = jax.ShapeDtypeStruct((count * padded, tokens), F32)
        block = pl.BlockSpec((pair * padded, tokens), lambda i, r: (i, 0))
    outs = 2 * steps if split else 2
    return pl.pallas_call(
        kernel,
        grid_spec=pltpu.PrefetchScalarGridSpec(
            num_scalar_prefetch=1,
            grid=(steps,),
            in_specs=[
                pl.BlockSpec((pair * step, 2, depth), place),
                pl.BlockSpec((tokens, depth), lambda i, r: (0, 0)),
            ],
            out_specs=[block] * outs,
            scratch_shapes=[pltpu.VMEM((tokens // 128, 2 * pair * step + 20, 128), F32)],
        ),
        out_shape=[out] * outs,
        compiler_params=params(50),
        cost_estimate=TINY,
    )(ids, head, rows)


def hits(ids_ref, targets_ref, shape):
    columns = ids_ref[4] + lax.broadcasted_iota(jnp.int32, shape, 0)
    return columns == targets_ref[...]


def student_product(head, own, other, targets, ids):
    width, depth = head.shape
    half = own.shape[0]
    tokens = 2 * half
    block = 256

    def kernel(ids_ref, w_ref, own_ref, other_ref, t_ref, s_ref, e_ref, out_ref, xs):
        g = ids_ref[0]
        xs[pl.ds(pl.multiple_of(g * half, half), half), :] = own_ref[...]
        xs[pl.ds(pl.multiple_of((1 - g) * half, half), half), :] = other_ref[...]
        for start in range(0, width, block):
            rows = slice(start, min(start + block, width))
            s_ref[rows, :] = lax.dot_general(
                w_ref[rows, :], xs[...], (((1,), (1,)), ((), ())), preferred_element_type=F32
            )
        s = s_ref[...]
        top = jnp.max(s, axis=0, keepdims=True)
        e = jnp.exp(s - top)
        e_ref[...] = e
        hit = hits(ids_ref, t_ref, s.shape)
        out_ref[...] = jnp.zeros_like(out_ref)
        out_ref[3:4, :] = top
        out_ref[4:5, :] = jnp.sum(e, axis=0, keepdims=True)
        out_ref[5:6, :] = jnp.sum(jnp.where(hit, s, jnp.zeros_like(s)), axis=0, keepdims=True)

    logits = jax.ShapeDtypeStruct((width, tokens), F32)
    return call(
        kernel,
        [logits, logits, jax.ShapeDtypeStruct((8, tokens), F32)],
        ids,
        head,
        own,
        other,
        targets,
        in_specs=[SMEM] + [VMEM] * 4,
        scratch=[pltpu.VMEM((tokens, depth), BF16)],
    )


def local_stats(mine, core, near, student, student_stats):
    width, tokens = student.shape
    step = width // BLOCKS
    padded = -(-step // 8) * 8

    def kernel(mine_ref, core_ref, *refs):
        near_refs = refs[: len(near)]
        s_ref, in_ref, te_ref, out_ref = refs[len(near) :]
        b = 0
        for ref in near_refs:
            for i in range(ref.shape[0] // padded):
                here = slice(b * padded, b * padded + step)
                there = slice(i * padded, i * padded + step)
                own = mine_ref[here, :] + core_ref[here, :]
                te_ref[b * step : (b + 1) * step, :] = own + ref[there, :]
                b += 1
        t = te_ref[...]
        top = jnp.max(t, axis=0, keepdims=True)
        e = jnp.exp(t - top)
        te_ref[...] = e
        out_ref[...] = in_ref[...]
        out_ref[0:1, :] = top
        out_ref[1:2, :] = jnp.sum(e, axis=0, keepdims=True)
        out_ref[2:3, :] = jnp.sum(e * (t - s_ref[...]), axis=0, keepdims=True)

    return call(
        kernel,
        [jax.ShapeDtypeStruct((width, tokens), F32), jax.ShapeDtypeStruct((8, tokens), F32)],
        mine,
        core,
        *near,
        student,
        student_stats,
    )


def merge(stats):
    def kernel(*refs):
        out_ref = refs[-1]
        values = [r[...] for r in refs[:-1]]

        def row(v, i):
            return v[i : i + 1, :]

        for top_row, sums in ((0, (1, 2)), (3, (4,))):
            top = functools.reduce(jnp.maximum, [row(v, top_row) for v in values])
            scale = [jnp.exp(row(v, top_row) - top) for v in values]
            out_ref[top_row : top_row + 1, :] = top
            for i in sums:
                out_ref[i : i + 1, :] = sum(c * row(v, i) for c, v in zip(scale, values))
        out_ref[5:6, :] = sum(row(v, 5) for v in values)
        out_ref[6:8, :] = values[0][6:8, :]

    return call(kernel, jax.ShapeDtypeStruct(stats[0].shape, F32), *stats)


def merge_all(stats):
    def kernel(in_ref, out_ref):
        for top_row, sums in ((0, (1, 2)), (3, (4,))):
            tops = in_ref[:, top_row, :]
            top = jnp.max(tops, axis=0, keepdims=True)
            scale = jnp.exp(tops - top)
            out_ref[top_row : top_row + 1, :] = top
            for i in sums:
                out_ref[i : i + 1, :] = jnp.sum(scale * in_ref[:, i, :], axis=0, keepdims=True)
        out_ref[5:6, :] = jnp.sum(in_ref[:, 5, :], axis=0, keepdims=True)
        out_ref[6:8, :] = jnp.zeros((2, in_ref.shape[2]), F32)

    return call(kernel, jax.ShapeDtypeStruct(stats.shape[1:], F32), stats)


def hidden_part(head, teacher, student, here, stats, targets, loss_grad, ids):
    width, depth = head.shape
    tokens = teacher.shape[1]
    half = tokens // 2
    block = 1024

    def kernel(
        ids_ref, w_ref, te_ref, se_ref, here_ref, st_ref, t_ref, g_ref, own_ref, other_ref, grad
    ):
        st, here = st_ref[...], here_ref[...]
        t_probs = te_ref[...] * (jnp.exp(here[0:1, :] - st[0:1, :]) / st[1:2, :])
        s_probs = se_ref[...] * (jnp.exp(here[3:4, :] - st[3:4, :]) / st[4:5, :])
        hit = hits(ids_ref, t_ref, t_probs.shape)
        value = g_ref[...] * (2.0 * s_probs - t_probs - hit.astype(F32))
        first = ids_ref[0] == 0
        low, high = value[:, :half].T, value[:, half:].T
        grad[0:half, :] = jnp.where(first, low, high).astype(BF16)
        grad[half:tokens, :] = jnp.where(first, high, low).astype(BF16)
        for start in range(0, depth, block):
            cols = slice(start, start + block)
            out = jnp.dot(grad[...], w_ref[:, cols], preferred_element_type=F32)
            own_ref[:, cols] = out[:half]
            other_ref[:, cols] = out[half:].astype(BF16)

    return call(
        kernel,
        [jax.ShapeDtypeStruct((half, depth), F32), jax.ShapeDtypeStruct((half, depth), BF16)],
        ids,
        head,
        teacher,
        student,
        here,
        stats,
        targets,
        loss_grad,
        in_specs=[SMEM] + [VMEM] * 7,
        scratch=[pltpu.VMEM((tokens, width), BF16)],
    )


def add_parts(own, other, blocks):
    tokens, depth = own.shape

    def kernel(own_ref, other_ref, out_ref):
        size = depth // 4
        for start in range(0, depth, size):
            cols = slice(start, start + size)
            total = (own_ref[:, cols] + other_ref[:, cols].astype(F32)).astype(BF16)
            out_ref[:, :, cols] = total.reshape(blocks, tokens // blocks, size)

    return call(kernel, jax.ShapeDtypeStruct((blocks, tokens // blocks, depth), BF16), own, other)


def sum_parts(parts):
    def kernel(in_ref, out_ref):
        total = in_ref[0].astype(F32)
        for i in range(1, in_ref.shape[0]):
            total += in_ref[i].astype(F32)
        out_ref[...] = total.astype(BF16)

    return call(kernel, jax.ShapeDtypeStruct(parts.shape[1:], BF16), parts)


def body(teacher_rows, student_rows, teacher_head, student_head, targets, loss_grad):
    t_head = jnp.transpose(teacher_head, (2, 1, 0))
    s_head = jnp.transpose(student_head, (1, 0))
    width = s_head.shape[0]
    grp, vocab, seq = lax.axis_index("grp"), lax.axis_index("vocab"), lax.axis_index("seq")
    shard = (grp * lax.axis_size("vocab") + vocab) * lax.axis_size("seq") + seq
    ids = jnp.stack([grp, seq, (vocab // 4) % 4, vocab % 4, shard * width]).astype(jnp.int32)
    targets2, loss_grad2 = targets.reshape(1, -1), loss_grad.reshape(1, -1)

    after = lax.optimization_barrier

    a = spread_rows(teacher_rows, lax.axis_size("vocab"))
    a, student_rows = after((a, student_rows))
    near_b = swap_xhi(student_rows)
    pair = [jnp.where(vocab < 16, p, q) for p, q in ((student_rows, near_b), (near_b, student_rows))]
    b = spread_rows(jnp.stack(pair), 16)
    a = lax.all_to_all(a, "vocab", 0, 0, tiled=True).reshape(-1, teacher_rows.shape[1])
    a, b = after((a, b))
    planes = [[x * 16 + i for i in range(16)] for x in range(2)]
    b = lax.all_to_all(b, "vocab", 0, 0, axis_index_groups=planes, tiled=True)

    own0, other0, own1, other1 = teacher_part(t_head, a, ids, False, 0, 4, split=True)
    sum0 = own0 + swap_core(other0)
    a, own1, other1, sum0 = after((a, own1, other1, sum0))
    near0 = swap_seq(sum0)
    sum1 = own1 + swap_core(other1)
    own2, other2 = teacher_part(t_head, a, ids, False, 4, 2)
    a, own2, other2, sum1, near0, b = after((a, own2, other2, sum1, near0, b))
    b = place(b)
    a, own2, other2, sum1, b = after((a, own2, other2, sum1, b))
    near1 = swap_seq(sum1)
    sum2 = own2 + swap_core(other2)
    b_other = swap_core(b)
    mine, other = teacher_part(t_head, a, ids, True, 0, BLOCKS)
    mine, other, b, b_other, sum2, near1 = after((mine, other, b, b_other, sum2, near1))
    near2 = swap_seq(sum2)
    core = swap_core(other)
    logits, student, student_stats = student_product(s_head, b, b_other, targets2, ids)
    near = [near0, near1, near2]
    teacher, here = local_stats(mine, core, near, logits, student_stats)
    stats = merge([here, swap_core(here)])
    stats = spread_rows(stats, 64)
    stats = merge_all(lax.all_to_all(stats, ("vocab", "seq"), 0, 0, tiled=True))

    own, other = hidden_part(s_head, teacher, student, here, stats, targets2, loss_grad2, ids)
    part = add_parts(own, swap_core(other), 64)
    part = lax.all_to_all(part, ("vocab", "seq"), 0, 0, tiled=True)
    hidden = sum_parts(part)

    t_norm = stats[0] + jnp.log(stats[1])
    s_norm = stats[3] + jnp.log(stats[4])
    token_loss = stats[2] / stats[1] - t_norm + 2.0 * s_norm - stats[5]
    return hidden, token_loss


def solution(mesh):
    return jax.shard_map(
        body,
        mesh=mesh,
        in_specs=(
            P("vocab", ("grp", "seq")),
            P(("grp", "vocab"), None),
            P(("grp", "seq"), None, "vocab"),
            P(None, ("grp", "vocab", "seq")),
            P(),
            P(),
        ),
        out_specs=(P(("grp", "vocab", "seq"), None), P()),
        check_vma=False,
    )
```

```python
import functools

import jax
import jax.numpy as jnp
from jax import lax
from jax.experimental import pallas as pl
from jax.experimental.pallas import tpu as pltpu
from jax.sharding import PartitionSpec as P

F32 = jnp.float32
BF16 = jnp.bfloat16
BLOCKS = 6
TINY = pl.CostEstimate(flops=1000, bytes_accessed=1000, transcendentals=0)
VMEM = pl.BlockSpec(memory_space=pltpu.VMEM)
SMEM = pl.BlockSpec(memory_space=pltpu.SMEM)


def params(mib=20):
    return pltpu.CompilerParams(vmem_limit_bytes=mib * 1024 * 1024)


def call(kernel, out_shape, *args, in_specs=None, scratch=(), mib=20):
    return pl.pallas_call(
        kernel,
        out_shape=out_shape,
        in_specs=in_specs or [VMEM] * len(args),
        out_specs=jax.tree.map(lambda _: VMEM, out_shape),
        scratch_shapes=scratch,
        compiler_params=params(mib),
        cost_estimate=TINY,
    )(*args)


def swap_xhi(a):
    return lax.ppermute(a, "vocab", [(i, i ^ 16) for i in range(32)])


def swap_core(a):
    return lax.ppermute(a, "grp", [(0, 1), (1, 0)])


def swap_seq(a):
    return lax.ppermute(a, "seq", [(0, 1), (1, 0)])


def spread_rows(rows, copies):
    def kernel(in_ref, out_ref):
        for i in range(copies):
            out_ref[i] = in_ref[...]

    return call(kernel, jax.ShapeDtypeStruct((copies,) + rows.shape, rows.dtype), rows)


def place(a):
    n, two, m, w = a.shape

    def kernel(in_ref, out_ref):
        for h in range(two):
            out_ref[h * n * m : (h + 1) * n * m, :] = in_ref[:, h].reshape(n * m, w)

    return call(kernel, jax.ShapeDtypeStruct((two * n * m, w), BF16), a)


def teacher_part(head, rows, ids, mine, first, count, split=False):
    width, _, depth = head.shape
    step = width // (2 * BLOCKS)
    tokens = rows.shape[0]
    padded = -(-step // 8) * 8
    pair = 2 if split else min(count, 3)
    steps = count // pair

    def place(i, ids_ref):
        part = ids_ref[1] if mine else 1 - ids_ref[1]
        return ((part * BLOCKS + first) // pair + i, 0, 0)

    def kernel(ids_ref, w_ref, x_ref, *refs):
        acc = refs[-1]
        g = ids_ref[0]
        w = w_ref[...].reshape(2 * pair * step, depth)
        out = lax.dot_general(w, x_ref[...], (((1,), (1,)), ((), ())), preferred_element_type=F32)
        for lane in range(tokens // 128):
            acc[lane, 0 : 2 * pair * step, :] = out[:, lane * 128 : lane * 128 + 128]

        def store(own_ref, other_ref):
            for lane in range(tokens // 128):
                cols = slice(lane * 128, lane * 128 + 128)
                for i in range(pair):
                    to = slice(i * padded, i * padded + step)
                    start = i * 2 * step
                    own_ref[to, cols] = acc[lane, pl.ds(start + g, step, stride=2), :]
                    other_ref[to, cols] = acc[lane, pl.ds(start + 1 - g, step, stride=2), :]

        if split:
            for j in range(steps):
                pl.when(pl.program_id(0) == j)(
                    functools.partial(store, refs[2 * j], refs[2 * j + 1])
                )
        else:
            store(refs[0], refs[1])

    if split:
        out = jax.ShapeDtypeStruct((pair * padded, tokens), F32)
        block = pl.BlockSpec((pair * padded, tokens), lambda i, r: (0, 0))
    else:
        out = jax.ShapeDtypeStruct((count * padded, tokens), F32)
        block = pl.BlockSpec((pair * padded, tokens), lambda i, r: (i, 0))
    outs = 2 * steps if split else 2
    return pl.pallas_call(
        kernel,
        grid_spec=pltpu.PrefetchScalarGridSpec(
            num_scalar_prefetch=1,
            grid=(steps,),
            in_specs=[
                pl.BlockSpec((pair * step, 2, depth), place),
                pl.BlockSpec((tokens, depth), lambda i, r: (0, 0)),
            ],
            out_specs=[block] * outs,
            scratch_shapes=[pltpu.VMEM((tokens // 128, 2 * pair * step + 20, 128), F32)],
        ),
        out_shape=[out] * outs,
        compiler_params=params(50),
        cost_estimate=TINY,
    )(ids, head, rows)


def hits(ids_ref, targets_ref, shape):
    columns = ids_ref[4] + lax.broadcasted_iota(jnp.int32, shape, 0)
    return columns == targets_ref[...]


def student_product(head, own, other, targets, ids):
    width, depth = head.shape
    half = own.shape[0]
    tokens = 2 * half
    block = 256

    def kernel(ids_ref, w_ref, own_ref, other_ref, t_ref, s_ref, e_ref, out_ref, xs):
        g = ids_ref[0]
        xs[pl.ds(pl.multiple_of(g * half, half), half), :] = own_ref[...]
        xs[pl.ds(pl.multiple_of((1 - g) * half, half), half), :] = other_ref[...]
        for start in range(0, width, block):
            rows = slice(start, min(start + block, width))
            s_ref[rows, :] = lax.dot_general(
                w_ref[rows, :], xs[...], (((1,), (1,)), ((), ())), preferred_element_type=F32
            )
        s = s_ref[...]
        top = jnp.max(s, axis=0, keepdims=True)
        e = jnp.exp(s - top)
        e_ref[...] = e
        hit = hits(ids_ref, t_ref, s.shape)
        out_ref[...] = jnp.zeros_like(out_ref)
        out_ref[3:4, :] = top
        out_ref[4:5, :] = jnp.sum(e, axis=0, keepdims=True)
        out_ref[5:6, :] = jnp.sum(jnp.where(hit, s, jnp.zeros_like(s)), axis=0, keepdims=True)

    logits = jax.ShapeDtypeStruct((width, tokens), F32)
    return call(
        kernel,
        [logits, logits, jax.ShapeDtypeStruct((8, tokens), F32)],
        ids,
        head,
        own,
        other,
        targets,
        in_specs=[SMEM] + [VMEM] * 4,
        scratch=[pltpu.VMEM((tokens, depth), BF16)],
    )


def local_stats(mine, core, near, student, student_stats):
    width, tokens = student.shape
    step = width // BLOCKS
    padded = -(-step // 8) * 8

    def kernel(mine_ref, core_ref, *refs):
        near_refs = refs[: len(near)]
        s_ref, in_ref, te_ref, out_ref = refs[len(near) :]
        b = 0
        for ref in near_refs:
            for i in range(ref.shape[0] // padded):
                here = slice(b * padded, b * padded + step)
                there = slice(i * padded, i * padded + step)
                own = mine_ref[here, :] + core_ref[here, :]
                te_ref[b * step : (b + 1) * step, :] = own + ref[there, :]
                b += 1
        t = te_ref[...]
        top = jnp.max(t, axis=0, keepdims=True)
        e = jnp.exp(t - top)
        te_ref[...] = e
        out_ref[...] = in_ref[...]
        out_ref[0:1, :] = top
        out_ref[1:2, :] = jnp.sum(e, axis=0, keepdims=True)
        out_ref[2:3, :] = jnp.sum(e * (t - s_ref[...]), axis=0, keepdims=True)

    return call(
        kernel,
        [jax.ShapeDtypeStruct((width, tokens), F32), jax.ShapeDtypeStruct((8, tokens), F32)],
        mine,
        core,
        *near,
        student,
        student_stats,
    )


def merge(stats, copies):
    def kernel(*refs):
        out_ref = refs[-1].at[0]
        values = [r[...] for r in refs[:-1]]

        def row(v, i):
            return v[i : i + 1, :]

        for top_row, sums in ((0, (1, 2)), (3, (4,))):
            top = functools.reduce(jnp.maximum, [row(v, top_row) for v in values])
            scale = [jnp.exp(row(v, top_row) - top) for v in values]
            out_ref[top_row : top_row + 1, :] = top
            for i in sums:
                out_ref[i : i + 1, :] = sum(c * row(v, i) for c, v in zip(scale, values))
        out_ref[5:6, :] = sum(row(v, 5) for v in values)
        out_ref[6:8, :] = values[0][6:8, :]
        merged = out_ref[...]
        for i in range(1, copies):
            refs[-1][i] = merged

    return call(kernel, jax.ShapeDtypeStruct((copies,) + stats[0].shape, F32), *stats)


def merge_all(stats):
    def kernel(in_ref, out_ref):
        for top_row, sums in ((0, (1, 2)), (3, (4,))):
            tops = in_ref[:, top_row, :]
            top = jnp.max(tops, axis=0, keepdims=True)
            scale = jnp.exp(tops - top)
            out_ref[top_row : top_row + 1, :] = top
            for i in sums:
                out_ref[i : i + 1, :] = jnp.sum(scale * in_ref[:, i, :], axis=0, keepdims=True)
        out_ref[5:6, :] = jnp.sum(in_ref[:, 5, :], axis=0, keepdims=True)
        out_ref[6:8, :] = jnp.zeros((2, in_ref.shape[2]), F32)

    return call(kernel, jax.ShapeDtypeStruct(stats.shape[1:], F32), stats)


def hidden_part(head, teacher, student, here, stats, targets, loss_grad, ids):
    width, depth = head.shape
    tokens = teacher.shape[1]
    half = tokens // 2
    block = 1024

    def kernel(
        ids_ref, w_ref, te_ref, se_ref, here_ref, st_ref, t_ref, g_ref, own_ref, other_ref, grad
    ):
        st, here = st_ref[...], here_ref[...]
        t_probs = te_ref[...] * (jnp.exp(here[0:1, :] - st[0:1, :]) / st[1:2, :])
        s_probs = se_ref[...] * (jnp.exp(here[3:4, :] - st[3:4, :]) / st[4:5, :])
        hit = hits(ids_ref, t_ref, t_probs.shape)
        value = g_ref[...] * (2.0 * s_probs - t_probs - hit.astype(F32))
        first = ids_ref[0] == 0
        low, high = value[:, :half].T, value[:, half:].T
        grad[0:half, :] = jnp.where(first, low, high).astype(BF16)
        grad[half:tokens, :] = jnp.where(first, high, low).astype(BF16)
        for start in range(0, depth, block):
            cols = slice(start, start + block)
            out = jnp.dot(grad[...], w_ref[:, cols], preferred_element_type=F32)
            own_ref[:, cols] = out[:half]
            other_ref[:, cols] = out[half:].astype(BF16)

    return call(
        kernel,
        [jax.ShapeDtypeStruct((half, depth), F32), jax.ShapeDtypeStruct((half, depth), BF16)],
        ids,
        head,
        teacher,
        student,
        here,
        stats,
        targets,
        loss_grad,
        in_specs=[SMEM] + [VMEM] * 7,
        scratch=[pltpu.VMEM((tokens, width), BF16)],
    )


def add_parts(own, other, blocks):
    tokens, depth = own.shape

    def kernel(own_ref, other_ref, out_ref):
        size = depth // 4
        for start in range(0, depth, size):
            cols = slice(start, start + size)
            total = (own_ref[:, cols] + other_ref[:, cols].astype(F32)).astype(BF16)
            out_ref[:, :, cols] = total.reshape(blocks, tokens // blocks, size)

    return call(kernel, jax.ShapeDtypeStruct((blocks, tokens // blocks, depth), BF16), own, other)


def sum_parts(parts):
    def kernel(in_ref, out_ref):
        total = in_ref[0].astype(F32)
        for i in range(1, in_ref.shape[0]):
            total += in_ref[i].astype(F32)
        out_ref[...] = total.astype(BF16)

    return call(kernel, jax.ShapeDtypeStruct(parts.shape[1:], BF16), parts)


def body(teacher_rows, student_rows, teacher_head, student_head, targets, loss_grad):
    t_head = jnp.transpose(teacher_head, (2, 1, 0))
    s_head = jnp.transpose(student_head, (1, 0))
    width = s_head.shape[0]
    grp, vocab, seq = lax.axis_index("grp"), lax.axis_index("vocab"), lax.axis_index("seq")
    shard = (grp * lax.axis_size("vocab") + vocab) * lax.axis_size("seq") + seq
    ids = jnp.stack([grp, seq, (vocab // 4) % 4, vocab % 4, shard * width]).astype(jnp.int32)
    targets2, loss_grad2 = targets.reshape(1, -1), loss_grad.reshape(1, -1)

    after = lax.optimization_barrier

    a = spread_rows(teacher_rows, lax.axis_size("vocab"))
    a, student_rows = after((a, student_rows))
    near_b = swap_xhi(student_rows)
    pair = [jnp.where(vocab < 16, p, q) for p, q in ((student_rows, near_b), (near_b, student_rows))]
    b = spread_rows(jnp.stack(pair), 16)
    a = lax.all_to_all(a, "vocab", 0, 0, tiled=True).reshape(-1, teacher_rows.shape[1])
    a, b = after((a, b))
    planes = [[x * 16 + i for i in range(16)] for x in range(2)]
    b = lax.all_to_all(b, "vocab", 0, 0, axis_index_groups=planes, tiled=True)

    own0, other0, own1, other1 = teacher_part(t_head, a, ids, False, 0, 4, split=True)
    sum0 = own0 + swap_core(other0)
    a, own1, other1, sum0 = after((a, own1, other1, sum0))
    near0 = swap_seq(sum0)
    sum1 = own1 + swap_core(other1)
    own2, other2 = teacher_part(t_head, a, ids, False, 4, 2)
    a, own2, other2, sum1, near0, b = after((a, own2, other2, sum1, near0, b))
    b = place(b)
    a, own2, other2, sum1, b = after((a, own2, other2, sum1, b))
    near1 = swap_seq(sum1)
    sum2 = own2 + swap_core(other2)
    b_other = swap_core(b)
    mine, other = teacher_part(t_head, a, ids, True, 0, BLOCKS)
    mine, other, b, b_other, sum2, near1 = after((mine, other, b, b_other, sum2, near1))
    near2 = swap_seq(sum2)
    core = swap_core(other)
    logits, student, student_stats = student_product(s_head, b, b_other, targets2, ids)
    near = [near0, near1, near2]
    teacher, here = local_stats(mine, core, near, logits, student_stats)
    stats = merge([here, swap_core(here)], 64)
    stats = merge_all(lax.all_to_all(stats, ("vocab", "seq"), 0, 0, tiled=True))

    own, other = hidden_part(s_head, teacher, student, here, stats, targets2, loss_grad2, ids)
    part = add_parts(own, swap_core(other), 64)
    part = lax.all_to_all(part, ("vocab", "seq"), 0, 0, tiled=True)
    hidden = sum_parts(part)

    t_norm = stats[0] + jnp.log(stats[1])
    s_norm = stats[3] + jnp.log(stats[4])
    token_loss = stats[2] / stats[1] - t_norm + 2.0 * s_norm - stats[5]
    return hidden, token_loss


def solution(mesh):
    return jax.shard_map(
        body,
        mesh=mesh,
        in_specs=(
            P("vocab", ("grp", "seq")),
            P(("grp", "vocab"), None),
            P(("grp", "seq"), None, "vocab"),
            P(None, ("grp", "vocab", "seq")),
            P(),
            P(),
        ),
        out_specs=(P(("grp", "vocab", "seq"), None), P()),
        check_vma=False,
    )
```
